32 devices in a mesh: row: 16 (over z, x, core), col: 2 (over y).
Axes of the slice: x: 2, y: 2, z: 4, core: 2. Of those that a mesh axis runs over, the one named last changes fastest.
Arguments:
- gbar: float32 [8192, 8192], P('row', 'col'), may hold values from -9 to 9, as said below
- panels: float32 [8192, 1024], P('row'), may hold values from -0.0625 to 0.0625
- panel_cot: float32 [8192, 1024], P('row'), may hold values from -6 to 6
- inverses: float32 [2, 512, 512], replicated, may hold values from -1 to 2, as said below
Outputs:
- adjoint: float32 [8192, 1024], P('row')
- diag_adjoint: float32 [2, 512, 512], P(None, 'row')
The draws below stay inside these ranges and needn't reach their ends.
Inputs may be any that keep to these rules, and one draw needn't show every extreme that they name: G, formed from gbar as in the reference program, is symmetric. Each inverses[i] is lower triangular with diagonal entries between 1 and 2.
All inputs are finite; a program needn't handle non-finite values.
Results may differ from the reference program's by a relative error of at most 0.000071.
Values sent between devices are 32-bit elements; how exact they have to be, the bound alone decides.
A program may use at most 128 MiB of HBM per device.

```python
import jax
import jax.numpy as jnp
from jax import lax

B = 512
NT = 16
KC = 8
M = 8192
N_COL = 2


def draw_gbar(key, part):
    order_total = NT * B
    raw = jnp.clip(jax.random.normal(key, (order_total, order_total), jnp.float32), -6.0, 6.0)
    symmetric = (raw + raw.T) * 0.70710678
    stored = symmetric.reshape(order_total, KC, NT // KC, B).transpose(0, 2, 1, 3).reshape(order_total, order_total)
    return stored


def draw_inverses(key, part):
    diag_key = jax.random.fold_in(key, 11)
    off_key = jax.random.fold_in(key, 23)
    diagonal = jax.random.uniform(diag_key, (2, B), jnp.float32, 1.0, 2.0)
    below = jnp.clip(jax.random.normal(off_key, (2, B, B), jnp.float32), -4.0, 4.0) * (0.6 / B ** 0.5)
    rows_idx = jnp.arange(B)[:, None]
    cols_idx = jnp.arange(B)[None, :]
    lower = jnp.where(rows_idx > cols_idx, 1.0, 0.0).astype(jnp.float32)
    eye_mat = jnp.where(rows_idx == cols_idx, 1.0, 0.0).astype(jnp.float32)
    return below * lower[None] + diagonal[:, :, None] * eye_mat[None]


def levels(own_key, shape, pieces, low, top_value):
    gain, own = 1.0, jax.random.fold_in(own_key, 6)
    for axis_at, blocks in pieces:
        steps = jnp.exp(jax.random.uniform(jax.random.fold_in(own, axis_at), (blocks,), jnp.float32, low / len(pieces), top_value / len(pieces)))
        gain = gain * jnp.repeat(steps, shape[axis_at] // blocks).reshape([-1 if axis == axis_at else 1 for axis in range(len(shape))])
    return gain


def normal_values(own_key, shape, deviation, limit, shards=(), held_as=jnp.bfloat16):
    result = deviation * jax.random.normal(own_key, shape, jnp.float32)
    if shards:
        result = result * levels(own_key, shape, shards, -0.22, 0.18)
    return jnp.clip(result, -limit, limit).astype(held_as)


def setup_inputs(seed: int = 0) -> dict:
    seeds = jax.random.split(jax.random.key(seed), 5)
    gbar = draw_gbar(jax.random.fold_in(seeds[4], 71), 0)
    panels = normal_values(seeds[1], (M, 2 * B), M ** -0.5, 0.0625, ((0, 16),), jnp.float32)
    panel_cot = normal_values(seeds[2], (M, 2 * B), 1.0, 6.0, ((0, 16),), jnp.float32)
    inverses = draw_inverses(jax.random.fold_in(seeds[4], 71), 0)
    return dict(gbar=gbar, panels=panels, panel_cot=panel_cot, inverses=inverses)


def reference(gbar, panels, panel_cot, inverses):
    width = inverses.shape[-1]
    order_total = panels.shape[0]
    exact_mode = lax.Precision.HIGHEST
    reordered = panels.reshape(KC, N_COL, width, 2 * width).transpose(1, 0, 2, 3).reshape(order_total, 2 * width)
    coupled = jnp.dot(gbar, reordered, precision=exact_mode, preferred_element_type=jnp.float32)
    combined = panel_cot - 2.0 * coupled
    first_adj = jnp.dot(combined[:, :width], inverses[0], precision=exact_mode, preferred_element_type=jnp.float32)
    second_adj = jnp.dot(combined[:, width:], inverses[1], precision=exact_mode, preferred_element_type=jnp.float32)
    adjoint = jnp.concatenate([first_adj, second_adj], axis=1)
    first_diag = -jnp.dot(first_adj.T, panels[:, :width], precision=exact_mode, preferred_element_type=jnp.float32)
    second_diag = -jnp.dot(second_adj.T, panels[:, width:], precision=exact_mode, preferred_element_type=jnp.float32)
    return adjoint, jnp.stack([first_diag, second_diag])
```

```python
import jax
import jax.numpy as jnp
from jax import lax
from jax.experimental import pallas as pl
from jax.experimental.pallas import tpu as pltpu
from jax.sharding import PartitionSpec as P

MESH = pl.DeviceIdType.MESH
SUBS = 4
UP, DOWN, ACROSS = 0, 1, 2


def halves(value):
    high = value.astype(jnp.bfloat16)
    low = (value - high.astype(jnp.float32)).astype(jnp.bfloat16)
    return high, low


def product(left, right):
    (left_high, left_low), (right_high, right_low) = left, right

    def one(a, b):
        return jnp.dot(a, b, preferred_element_type=jnp.float32)

    return one(left_high, right_low) + one(left_low, right_high) + one(left_high, right_high)


def ladder_kernel(
    nz, gbar, panels, cot, inverses,
    adjoint, diag,
    g_v, p_v, gath, terms, other, zin_pair, zin_one, xin_one, xin_last, final,
    acc, acc_other, p_high, p_low, inv_v, cot_t, adj_v,
    diag_v, diag_mate, diag_parts, diag_out,
    load_sems, own_sems, out_sems,
    gath_send, gath_far, gath_recv, gath_mate,
    term_sems, xone_sems, pair_send, pair_recv, one_send, one_recv, last_sems,
    end_send, end_recv, acc_sems,
    mate_sems, part_send, part_recv, swap_sems,
):
    width = inverses.shape[-1]
    chips = 2 * nz
    half = width // 2
    lane = width // 4
    piece = lane // SUBS
    row = lax.axis_index("row")
    col = lax.axis_index("col")
    chip = row // 2
    core = row % 2
    mate = 1 - core
    x = chip % 2
    z = chip // 2
    across = 2 * z + 1 - x

    def port_chip(port):
        if port == ACROSS:
            return across
        return chip + 2 - 4 * port

    def has_next(port):
        return jnp.where(port == UP, z < nz - 1, z > 0)

    def has_prev(port):
        return jnp.where(port == UP, z > 0, z < nz - 1)

    def behind(port, step):
        return z - step + 2 * step * port

    def ahead(port, step):
        return z + step - 2 * step * port

    def inside(place):
        return (place >= 0) & (place < nz)

    def load_g(tile):
        start = pl.multiple_of(tile * width, width)
        return pltpu.make_async_copy(gbar.at[:, pl.ds(start, width)], g_v.at[tile], load_sems.at[tile])

    def load_p(panel):
        columns = slice(panel * width, (panel + 1) * width)
        return pltpu.make_async_copy(panels.at[:, columns], p_v.at[:, columns], load_sems.at[chips + panel])

    def load_own(side):
        columns = slice(side * half, (side + 1) * half)
        return pltpu.make_async_copy(panels.at[:, columns], gath.at[chip, side], own_sems.at[side])

    load_cot = pltpu.make_async_copy(cot, adj_v, load_sems.at[chips + 2])
    load_inv = pltpu.make_async_copy(inverses, inv_v, load_sems.at[chips + 3])

    def order(count):
        place = jnp.where(z < nz // 2, nz - 1 - count // 2, count // 2)
        return 2 * place + jnp.where(count % 2 == 0, 1 - x, x)

    @pl.when(core == col)
    def _():
        load_own(1).start()
        load_own(0).start()

    load_p(1).start()
    for count in range(chips):
        load_g(order(count)).start()
    load_p(0).start()
    load_cot.start()
    load_inv.start()

    barrier = pltpu.get_barrier_semaphore()
    friends = [(2 * ((chip + hop) % chips) + lead, col) for hop in range(1, chips) for lead in (0, 1)] + [
        (2 * chip + mate, col),
        (2 * chip + core, 1 - col),
        (2 * chip + mate, 1 - col),
    ]
    for friend in friends:
        pl.semaphore_signal(barrier, inc=1, device_id=friend, device_id_type=MESH)

    load_p(1).wait()
    for part in (0, 1):
        rows = slice(part * half, (part + 1) * half)
        high, low = halves(p_v[:, width + part * half:width + (part + 1) * half].T)
        p_high[rows, :] = high
        p_low[rows, :] = low
    pl.semaphore_wait(barrier, len(friends))

    def gather_copy(tile, side, port, lead, far):
        rows = pl.ds(pl.multiple_of(lead * half, half), half)
        return pltpu.make_async_remote_copy(
            gath.at[tile, side, rows],
            gath.at[tile, side, rows],
            gath_far.at[port, side] if far else gath_send.at[port, tile, side],
            gath_recv.at[tile, side],
            device_id=(2 * port_chip(port) + lead, col),
            device_id_type=MESH,
        )

    def gather_pair(tile, side):
        rows = pl.ds(pl.multiple_of(core * half, half), half)
        return pltpu.make_async_remote_copy(
            gath.at[tile, side, rows],
            gath.at[tile, side, rows],
            gath_mate.at[0, tile, side],
            gath_mate.at[1, tile, side],
            device_id=(2 * chip + mate, col),
            device_id_type=MESH,
        )

    def gather_own_pair(side):
        return pltpu.make_async_remote_copy(
            gath.at[chip, side],
            gath.at[chip, side],
            gath_mate.at[0, chip, side],
            gath_mate.at[1, chip, side],
            device_id=(2 * chip + mate, col),
            device_id_type=MESH,
        )

    def own_sends(act):
        def one(side, port):
            def go():
                act(gather_copy(chip, side, port, core, False))
                act(gather_copy(chip, side, port, mate, True))

            if port == ACROSS:
                go()
            else:
                pl.when(has_next(port))(go)

        @pl.when(core == col)
        def _():
            one(0, ACROSS)
            for side in (1, 0):
                for port in (UP, DOWN):
                    one(side, port)
            one(1, ACROSS)
            act(gather_own_pair(0))
            act(gather_own_pair(1))

    def relay(tile, side, ports, act):
        for port in ports:
            if port == ACROSS:
                act(gather_copy(tile, side, port, core, False))
            else:
                @pl.when(has_next(port))
                def _():
                    act(gather_copy(tile, side, port, core, False))
        act(gather_pair(tile, side))

    def arrived(tile, side):
        gather_copy(tile, side, ACROSS, core, False).wait_recv()

    def start(copy):
        copy.start()

    def finish(copy):
        copy.wait_send()

    def relay_b(step, act):
        for port in (UP, DOWN):
            place = behind(port, step)

            @pl.when(inside(place))
            def _():
                tile = 2 * place + x
                if act is start:
                    arrived(tile, 1)
                relay(tile, 1, (port, ACROSS), act)

    def relay_a(step, act, own):
        for port in (UP, DOWN):
            place = behind(port, step)

            @pl.when(inside(place))
            def _():
                tile = 2 * place + (x if own else 1 - x)
                if act is start:
                    arrived(tile, 0)
                relay(tile, 0, (port,), act)

    def relay_a_across(act):
        if act is start:
            arrived(across, 0)
        relay(across, 0, (UP, DOWN), act)

    def relay_bx(step, act):
        for port in (UP, DOWN) if step else (UP,):
            place = behind(port, step)

            @pl.when(inside(place))
            def _():
                tile = 2 * place + 1 - x
                if act is start:
                    arrived(tile, 1)
                relay(tile, 1, (), act)

    def forward(tile, side):
        @pl.when((tile != chip) | (core != col))
        def _():
            gather_pair_wait(tile, side)

        acc[side] += product(halves(g_v[tile]), halves(gath[tile, side]))

    def gather_pair_wait(tile, side):
        @pl.when(tile == chip)
        def _():
            gather_own_pair(side).wait_recv()

        @pl.when(tile != chip)
        def _():
            gather_pair(tile, side).wait_recv()

    def forward_step(step, kinds):
        def both(port, carry):
            place = behind(port, step)

            @pl.when(inside(place))
            def _():
                for side, own in kinds:
                    forward(2 * place + (x if own else 1 - x), side)

            return carry

        lax.fori_loop(0, 2 if step else 1, both, 0)

    def term_copy(tile):
        return pltpu.make_async_remote_copy(
            terms.at[tile, :, mate],
            other.at[tile],
            term_sems.at[0, tile],
            term_sems.at[1, tile],
            device_id=(2 * chip + mate, col),
            device_id_type=MESH,
        )

    def xone_copy(place, tile):
        return pltpu.make_async_remote_copy(
            terms.at[tile, 1, core],
            xin_one.at[place],
            xone_sems.at[0, place],
            xone_sems.at[1, place],
            device_id=(2 * across + core, col),
            device_id_type=MESH,
        )

    def make_terms(count):
        tile = order(count)
        load_g(tile).wait()
        for part in (0, 1):
            rows = slice(part * half, (part + 1) * half)
            value = product((p_high[rows, :], p_low[rows, :]), halves(g_v[tile]))
            terms[tile, part] = value.reshape(2, lane, width)
        term_copy(tile).start()

    def pair_terms(count):
        tile = order(count)
        term_copy(tile).wait_recv()
        terms[tile, :, core] = terms[tile, :, core] + other[tile]

        @pl.when(count == 0)
        def _():
            xone_copy(tile // 2, tile).start()

    def send_across(count):
        tile = order(count)
        xone_copy(tile // 2, tile).start()

    def pair_copy(port, step, slot, tile, sub):
        rows = pl.ds(sub * piece, piece)
        return pltpu.make_async_remote_copy(
            terms.at[tile, 0, core, rows],
            zin_pair.at[port, step - 1, slot, rows],
            pair_send.at[port, step - 1, slot, sub],
            pair_recv.at[port, step - 1, slot, sub],
            device_id=(2 * port_chip(port) + core, col),
            device_id_type=MESH,
        )

    def one_copy(port, step, tile, sub):
        rows = pl.ds(sub * piece, piece)
        return pltpu.make_async_remote_copy(
            terms.at[tile, 1, core, rows],
            zin_one.at[port, step - 1, rows],
            one_send.at[port, step - 1, sub],
            one_recv.at[port, step - 1, sub],
            device_id=(2 * port_chip(port) + core, col),
            device_id_type=MESH,
        )

    def sum_pair(step):
        for slot in (0, 1):
            for port in (UP, DOWN):
                place = ahead(port, step)

                @pl.when(inside(place))
                def _():
                    tile = 2 * place + (x if slot else 1 - x)

                    def each(sub, carry):
                        rows = pl.ds(pl.multiple_of(sub * piece, piece), piece)
                        if step < nz - 1:
                            @pl.when(has_prev(port))
                            def _():
                                pair_copy(port, step + 1, slot, tile, sub).wait_recv()
                                terms[tile, 0, core, rows] = (
                                    terms[tile, 0, core, rows] + zin_pair[port, step, slot, rows]
                                )

                        pair_copy(port, step, slot, tile, sub).start()
                        return carry

                    lax.fori_loop(0, SUBS, each, 0)

    def sum_one(step):
        for port in (UP, DOWN):
            place = ahead(port, step)

            @pl.when(inside(place))
            def _():
                tile = 2 * place + x
                xone_copy(place, tile).wait_recv()

                def each(sub, carry):
                    rows = pl.ds(pl.multiple_of(sub * piece, piece), piece)
                    value = terms[tile, 1, core, rows] + xin_one[place, rows]
                    terms[tile, 1, core, rows] = value
                    if step < nz - 1:
                        @pl.when(has_prev(port))
                        def _():
                            one_copy(port, step + 1, tile, sub).wait_recv()
                            terms[tile, 1, core, rows] = value + zin_one[port, step, rows]

                    one_copy(port, step, tile, sub).start()
                    return carry

                lax.fori_loop(0, SUBS, each, 0)

    def last_copy(sub):
        rows = pl.ds(sub * piece, piece)
        return pltpu.make_async_remote_copy(
            terms.at[across, 0, core, rows],
            xin_last.at[rows],
            last_sems.at[0, sub],
            last_sems.at[1, sub],
            device_id=(2 * across + core, col),
            device_id_type=MESH,
        )

    def end_copy(part, plane, source_core, sub):
        rows = pl.ds(sub * piece, piece)
        return pltpu.make_async_remote_copy(
            terms.at[chip, part, source_core, rows],
            final.at[part, source_core, rows],
            end_send.at[part, plane, sub],
            end_recv.at[part, source_core, sub],
            device_id=(2 * chip + col, col if plane == 0 else 1 - col),
            device_id_type=MESH,
        )

    def end_local(part, source_core, sub):
        rows = pl.ds(sub * piece, piece)
        return pltpu.make_async_copy(
            terms.at[chip, part, source_core, rows],
            final.at[part, source_core, rows],
            end_recv.at[part, source_core, sub],
        )

    def give_end(part, sub):
        end_copy(part, 1, core, sub).start()

        @pl.when(core == col)
        def _():
            end_local(part, core, sub).start()

        @pl.when(core != col)
        def _():
            end_copy(part, 0, core, sub).start()

    def last_pair(sub, carry):
        rows = pl.ds(pl.multiple_of(sub * piece, piece), piece)
        for slot in (0, 1):
            tile = chip if slot else across
            for port in (UP, DOWN):
                @pl.when(has_prev(port))
                def _():
                    pair_copy(port, 1, slot, tile, sub).wait_recv()
                    terms[tile, 0, core, rows] = terms[tile, 0, core, rows] + zin_pair[port, 0, slot, rows]

            if slot == 0:
                last_copy(sub).start()
        return carry

    def last_across(sub, carry):
        rows = pl.ds(pl.multiple_of(sub * piece, piece), piece)
        last_copy(sub).wait_recv()
        terms[chip, 0, core, rows] = terms[chip, 0, core, rows] + xin_last[rows]
        give_end(0, sub)
        return carry

    def last_one(sub, carry):
        rows = pl.ds(pl.multiple_of(sub * piece, piece), piece)
        terms[chip, 1, core, rows] = terms[chip, 1, core, rows] + xin_one[z, rows]
        for port in (UP, DOWN):
            @pl.when(has_prev(port))
            def _():
                one_copy(port, 1, chip, sub).wait_recv()
                terms[chip, 1, core, rows] = terms[chip, 1, core, rows] + zin_one[port, 0, rows]

        give_end(1, sub)
        return carry

    def acc_copy(side):
        return pltpu.make_async_remote_copy(
            acc.at[side],
            acc_other.at[side],
            acc_sems.at[0, side],
            acc_sems.at[1, side],
            device_id=(2 * chip + core, 1 - col),
            device_id_type=MESH,
        )

    side_columns = pl.ds(pl.multiple_of(col * half, half), half)
    short = width // (2 * chips)

    def mate_copy(panel):
        return pltpu.make_async_remote_copy(
            diag_v.at[panel, :, mate],
            diag_mate.at[panel],
            mate_sems.at[0, panel],
            mate_sems.at[1, panel],
            device_id=(2 * chip + mate, col),
            device_id_type=MESH,
        )

    def part_copy(panel, source, target):
        return pltpu.make_async_remote_copy(
            diag_v.at[panel, target, core],
            diag_parts.at[panel, source],
            part_send.at[panel, target],
            part_recv.at[panel, source],
            device_id=(2 * target + core, col),
            device_id_type=MESH,
        )

    def swap_copy(panel):
        return pltpu.make_async_remote_copy(
            diag_out.at[panel, :, side_columns],
            diag_out.at[panel, :, side_columns],
            swap_sems.at[0, panel],
            swap_sems.at[1, panel],
            device_id=(2 * chip + core, 1 - col),
            device_id_type=MESH,
        )

    def adjoint_out(panel):
        columns = slice(panel * width, (panel + 1) * width)
        return pltpu.make_async_copy(adj_v.at[:, columns], adjoint.at[:, columns], out_sems.at[panel])

    def solve_first():
        for side in (0, 1):
            acc_copy(side).wait_recv()
        for side in (0, 1):
            columns = slice(side * half, (side + 1) * half)
            cot_t[0, :, columns] = adj_v[:, columns] - 2.0 * (acc[side] + acc_other[side])
        turned = product(halves(cot_t[0]), halves(inv_v[0]))
        adj_v[:, :width] = turned
        adjoint_out(0).start()
        cot_t[0] = turned.T

    def solve_second():
        for part in (0, 1):
            for source in (0, 1):
                for sub in range(SUBS):
                    end_local(part, source, sub).wait()
        coupled = final[...].reshape(width, width)
        cot_t[1] = product(halves(inv_v[1]), halves(cot_t[1] - 2.0 * coupled))

    def diagonal(panel):
        place = pl.multiple_of(panel * width + col * half, half)
        own = p_v[:, pl.ds(place, half)]
        value = -product(halves(cot_t[panel]), halves(own))
        diag_v[panel] = value.reshape(chips, 2, short, half)
        mate_copy(panel).start()

    def give_second():
        adj_v[:, width:] = cot_t[1].T
        adjoint_out(1).start()

    def scatter(panel):
        mate_copy(panel).wait_recv()
        diag_v[panel, :, core] = diag_v[panel, :, core] + diag_mate[panel]
        for hop in range(1, chips):
            part_copy(panel, chip, (chip + hop) % chips).start()

    def collect(panel):
        total = diag_v[panel, chip, core]
        for hop in range(1, chips):
            source = (chip + hop) % chips
            part_copy(panel, source, chip).wait_recv()
            total = total + diag_parts[panel, source]
        diag_out[panel, :, side_columns] = total
        swap_copy(panel).start()

    def turn_cot():
        cot_t[1] = adj_v[:, width:].T

    def turn_inv():
        inv_v[1] = inv_v[1].T

    @pl.when(core == col)
    def _():
        load_own(1).wait()
        load_own(0).wait()

    own_sends(start)
    acc[...] = jnp.zeros_like(acc)
    chores = {
        4: lambda: relay_a_across(start),
        7: lambda: relay_b(1, start),
    }

    def produce(count, carry):
        make_terms(count)
        pl.when(count > 0)(lambda: pair_terms(count - 1))
        for at, chore in chores.items():
            pl.when(count == at)(chore)
        return carry

    lax.fori_loop(0, chips, produce, 0)
    pair_terms(jnp.int32(chips - 1))

    relay_a(1, start, True)
    sum_pair(3)
    forward_step(0, [(0, True), (1, True)])
    forward_step(1, [(0, True), (1, True)])
    relay_b(2, start)
    sum_one(3)
    relay_a(1, start, False)
    forward_step(1, [(0, False)])
    forward_step(0, [(0, False)])
    send_across(2)
    sum_pair(2)
    relay_b(3, start)
    forward_step(2, [(1, True)])
    relay_a(2, start, True)
    send_across(4)
    forward_step(2, [(0, True)])
    forward_step(3, [(1, True)])
    relay_bx(0, start)
    relay_bx(1, start)
    forward_step(0, [(1, False)])
    forward_step(1, [(1, False)])
    relay_a(2, start, False)
    sum_one(2)
    relay_bx(2, start)
    relay_bx(3, start)
    forward_step(2, [(1, False)])
    forward_step(3, [(1, False)])
    acc_copy(1).start()
    send_across(6)
    forward_step(2, [(0, False)])
    sum_pair(1)
    load_p(0).wait()
    load_cot.wait()
    load_inv.wait()
    turn_cot()
    turn_inv()
    relay_a(3, start, True)
    relay_a(3, start, False)
    forward_step(3, [(0, True), (0, False)])
    acc_copy(0).start()
    sum_one(1)
    lax.fori_loop(0, SUBS, last_pair, 0)
    lax.fori_loop(0, SUBS, last_across, 0)
    xone_copy(z, chip).wait_recv()
    lax.fori_loop(0, SUBS, last_one, 0)
    solve_first()
    diagonal(0)
    scatter(0)
    solve_second()
    diagonal(1)
    collect(0)
    scatter(1)
    give_second()
    collect(1)

    own_sends(finish)
    relay_a_across(finish)
    relay_bx(0, finish)

    def drain_terms(count, carry):
        tile = order(count)
        term_copy(tile).wait_send()

        @pl.when(tile % 2 != x)
        def _():
            xone_copy(tile // 2, tile).wait_send()

        return carry

    lax.fori_loop(0, chips, drain_terms, 0)
    for step in range(1, nz):
        relay_b(step, finish)
        relay_a(step, finish, True)
        relay_a(step, finish, False)
        relay_bx(step, finish)
        for port in (UP, DOWN):
            place = ahead(port, step)

            @pl.when(inside(place))
            def _():
                for sub in range(SUBS):
                    for slot in (0, 1):
                        pair_copy(port, step, slot, 2 * place + (x if slot else 1 - x), sub).wait_send()
                    one_copy(port, step, 2 * place + x, sub).wait_send()

    for sub in range(SUBS):
        last_copy(sub).wait_send()
        for part in (0, 1):
            end_copy(part, 1, core, sub).wait_send()

            @pl.when(core != col)
            def _():
                end_copy(part, 0, core, sub).wait_send()

    for panel in (0, 1):
        acc_copy(panel).wait_send()
        mate_copy(panel).wait_send()
        for hop in range(1, chips):
            part_copy(panel, chip, (chip + hop) % chips).wait_send()
        swap_copy(panel).wait()
        adjoint_out(panel).wait()
    store = pltpu.make_async_copy(diag_out, diag, out_sems.at[2])
    store.start()
    store.wait()


def ladder_device(gbar, panels, panel_cot, inverses):
    width = inverses.shape[-1]
    chips = lax.axis_size("row") // 2
    nz = chips // 2
    half, lane = width // 2, width // 4
    short = width // (2 * chips)
    f32, bf16, dma = jnp.float32, jnp.bfloat16, pltpu.SemaphoreType.DMA
    anywhere = pl.BlockSpec(memory_space=pl.ANY)

    def kernel(*refs):
        ladder_kernel(nz, *refs)

    return pl.pallas_call(
        kernel,
        out_shape=(
            jax.ShapeDtypeStruct(panels.shape, f32),
            jax.ShapeDtypeStruct((2, short, width), f32),
        ),
        in_specs=[anywhere] * 4,
        out_specs=(anywhere, anywhere),
        scratch_shapes=[
            pltpu.VMEM((chips, width, width), f32),
            pltpu.VMEM(panels.shape, f32),
            pltpu.VMEM((chips, 2, width, half), f32),
            pltpu.VMEM((chips, 2, 2, lane, width), f32),
            pltpu.VMEM((chips, 2, lane, width), f32),
            pltpu.VMEM((2, nz - 1, 2, lane, width), f32),
            pltpu.VMEM((2, nz - 1, lane, width), f32),
            pltpu.VMEM((nz, lane, width), f32),
            pltpu.VMEM((lane, width), f32),
            pltpu.VMEM((2, 2, lane, width), f32),
            pltpu.VMEM((2, width, half), f32),
            pltpu.VMEM((2, width, half), f32),
            pltpu.VMEM((width, width), bf16),
            pltpu.VMEM((width, width), bf16),
            pltpu.VMEM(inverses.shape, f32),
            pltpu.VMEM(inverses.shape, f32),
            pltpu.VMEM(panels.shape, f32),
            pltpu.VMEM((2, chips, 2, short, half), f32),
            pltpu.VMEM((2, chips, short, half), f32),
            pltpu.VMEM((2, chips, short, half), f32),
            pltpu.VMEM((2, short, width), f32),
            dma((chips + 4,)),
            dma((2,)),
            dma((3,)),
            dma((3, chips, 2)),
            dma((3, 2)),
            dma((chips, 2)),
            dma((2, chips, 2)),
            dma((2, chips)),
            dma((2, nz)),
            dma((2, nz - 1, 2, SUBS)),
            dma((2, nz - 1, 2, SUBS)),
            dma((2, nz - 1, SUBS)),
            dma((2, nz - 1, SUBS)),
            dma((2, SUBS)),
            dma((2, 2, SUBS)),
            dma((2, 2, SUBS)),
            dma((2, 2)),
            dma((2, 2)),
            dma((2, chips)),
            dma((2, chips)),
            dma((2, 2)),
        ],
        compiler_params=pltpu.CompilerParams(
            collective_id=0, has_side_effects=True, vmem_limit_bytes=62 * 1024 * 1024
        ),
    )(gbar, panels, panel_cot, inverses)


def plain_device(gbar, panels, panel_cot, inverses):
    width = inverses.shape[-1]
    mode = lax.Precision.HIGHEST
    row_id = lax.axis_index("row")
    col_count = lax.axis_size("col")
    contract = (((0,), (0,)), ((), ()))
    partial_value = lax.dot_general(
        gbar, panels, contract, precision=mode, preferred_element_type=jnp.float32
    )
    summed = lax.psum(partial_value, "row")
    own_tile = lax.dynamic_slice_in_dim(summed, row_id // col_count * width, width, 0)
    own_tile = jnp.where(lax.axis_index("col") == row_id % col_count, own_tile, 0)
    combined = panel_cot - 2.0 * lax.psum(own_tile, "col")
    adjoint, terms = [], []
    for panel in (0, 1):
        columns = slice(panel * width, (panel + 1) * width)
        adjoint.append(
            jnp.dot(combined[:, columns], inverses[panel], precision=mode, preferred_element_type=jnp.float32)
        )
        terms.append(
            -lax.dot_general(
                adjoint[-1], panels[:, columns], contract, precision=mode, preferred_element_type=jnp.float32
            )
        )
    diag_adjoint = lax.psum_scatter(jnp.stack(terms), "row", scatter_dimension=1, tiled=True)
    return jnp.concatenate(adjoint, axis=1), diag_adjoint


def solution(mesh):
    in_specs = (P("row", "col"), P("row", None), P("row", None), P())
    out_specs = (P("row", None), P(None, "row", None))
    on_ladder = mesh.shape["col"] == 2 and mesh.shape["row"] == 16
    return jax.shard_map(
        ladder_device if on_ladder else plain_device,
        mesh=mesh, in_specs=in_specs, out_specs=out_specs, check_vma=False,
    )
```

```python
import jax
import jax.numpy as jnp
from jax import lax
from jax.experimental import pallas as pl
from jax.experimental.pallas import tpu as pltpu
from jax.sharding import PartitionSpec as P

MESH = pl.DeviceIdType.MESH
SUBS = 4
UP, DOWN, ACROSS = 0, 1, 2
EARLY, COMB, LATE = 0, 1, 2
PAIRED = 96


def halves(value):
    high = value.astype(jnp.bfloat16)
    low = (value - high.astype(jnp.float32)).astype(jnp.bfloat16)
    return high, low


def product(left, right):
    (left_high, left_low), (right_high, right_low) = left, right

    def one(a, b):
        return jnp.dot(a, b, preferred_element_type=jnp.float32)

    return one(left_high, right_low) + one(left_low, right_high) + one(left_high, right_high)


def ladder_kernel(
    nz, gbar, panels, cot, inverses,
    adjoint, diag,
    g_v, p_v, gath_spine, gath_comb, terms, other, zin_pair, zin_one, xin_one, xin_last, final,
    acc_spine, acc_comb, acc_spine_other, acc_comb_other, p_high, p_low, inv_v, cot_t, adj_v,
    diag_v, diag_mate, diag_parts, diag_out,
    load_sems, own_sems, out_sems,
    gath_send, gath_recv, gath_mate,
    term_sems, xone_sems, pair_send, pair_recv, one_send, one_recv, last_sems,
    end_send, end_recv, acc_sems,
    mate_sems, part_send, part_recv, swap_sems,
):
    width = inverses.shape[-1]
    chips = 2 * nz
    half = width // 2
    lane = half
    row = lax.axis_index("row")
    col = lax.axis_index("col")
    chip = row // 2
    core = row % 2
    mate = 1 - core
    x = chip % 2
    z = chip // 2
    across = 2 * z + 1 - x

    def port_chip(port):
        if isinstance(port, int) and port == ACROSS:
            return across
        return chip + 2 - 4 * port

    def has_next(port):
        return jnp.where(port == UP, z < nz - 1, z > 0)

    def has_prev(port):
        return jnp.where(port == UP, z > 0, z < nz - 1)

    def behind(port, step):
        return z - step + 2 * step * port

    def ahead(port, step):
        return z + step - 2 * step * port

    def inside(place):
        return (place >= 0) & (place < nz)

    def load_g(tile):
        start = pl.multiple_of(tile * width, width)
        return pltpu.make_async_copy(gbar.at[:, pl.ds(start, width)], g_v.at[tile], load_sems.at[tile])

    def load_p(panel):
        columns = slice(panel * width, (panel + 1) * width)
        return pltpu.make_async_copy(panels.at[:, columns], p_v.at[:, columns], load_sems.at[chips + panel])

    def columns_of(side):
        quarter = width // 4
        return {EARLY: slice(0, quarter), LATE: slice(quarter, half), COMB: slice(half, width)}[side]

    def gath(tile, side):
        return gath_comb.at[tile] if side == COMB else gath_spine.at[side // 2, tile]

    def acc(side):
        return acc_comb if side == COMB else acc_spine.at[side // 2]

    def acc_other(side):
        return acc_comb_other if side == COMB else acc_spine_other.at[side // 2]

    def load_own(side):
        return pltpu.make_async_copy(panels.at[:, columns_of(side)], gath(chip, side), own_sems.at[side])

    load_cot = pltpu.make_async_copy(cot, adj_v, load_sems.at[chips + 2])
    load_inv = pltpu.make_async_copy(inverses, inv_v, load_sems.at[chips + 3])

    def order(count):
        place = jnp.where(z < nz // 2, nz - 1 - count // 2, count // 2)
        return 2 * place + jnp.where(count % 2 == 0, 1 - x, x)

    @pl.when(core == col)
    def _():
        for side in (EARLY, COMB, LATE):
            load_own(side).start()

    load_p(1).start()
    for count in range(chips):
        load_g(order(count)).start()
    load_p(0).start()
    load_cot.start()
    load_inv.start()

    barrier = pltpu.get_barrier_semaphore()
    friends = [
        (2 * across + core, col),
        (2 * chip + mate, col),
        (2 * chip + core, 1 - col),
        (2 * chip + mate, 1 - col),
    ]

    def greet(friend):
        pl.semaphore_signal(barrier, inc=1, device_id=friend, device_id_type=MESH)

    for friend in friends:
        greet(friend)
    for port in (UP, DOWN):
        pl.when(has_next(port))(lambda: greet((2 * port_chip(port) + core, col)))

    pl.semaphore_wait(barrier, len(friends) + jnp.where((z > 0) & (z < nz - 1), 2, 1))

    def gather_copy(tile, side, port):
        rows = pl.ds(pl.multiple_of(core * half, half), half)
        return pltpu.make_async_remote_copy(
            gath(tile, side).at[rows],
            gath(tile, side).at[rows],
            gath_send.at[port, tile, side],
            gath_recv.at[tile, side],
            device_id=(2 * port_chip(port) + core, col),
            device_id_type=MESH,
        )

    def gather_pair(tile, side):
        rows = pl.ds(pl.multiple_of(core * half, half), half)
        return pltpu.make_async_remote_copy(
            gath(tile, side).at[rows],
            gath(tile, side).at[rows],
            gath_mate.at[0, tile, side],
            gath_mate.at[1, tile, side],
            device_id=(2 * chip + mate, col),
            device_id_type=MESH,
        )

    def gather_own_pair(side):
        return pltpu.make_async_remote_copy(
            gath(chip, side),
            gath(chip, side),
            gath_mate.at[0, chip, side],
            gath_mate.at[1, chip, side],
            device_id=(2 * chip + mate, col),
            device_id_type=MESH,
        )

    def own_sends(act, routes, sides):
        @pl.when(core == col)
        def _():
            for side in sides:
                act(gather_own_pair(side))

        for side, port in routes:
            if side in sides and act is start:
                @pl.when(core != col)
                def _():
                    gather_own_pair(side).wait_recv()

                sides = tuple(other for other in sides if other != side)
            copy = gather_copy(chip, side, port)
            if port == ACROSS:
                act(copy)
            else:
                pl.when(has_next(port))(lambda: act(copy))

    first_routes = [(EARLY, ACROSS), (COMB, UP), (COMB, DOWN), (EARLY, UP), (EARLY, DOWN), (COMB, ACROSS)]

    def own_first(act):
        own_sends(act, first_routes, (EARLY, COMB))

    def own_across(act):
        own_sends(act, [(LATE, ACROSS)], (LATE,))

    def own_along(act):
        own_sends(act, [(LATE, UP), (LATE, DOWN)], ())

    def relay(tile, side, ports, act):
        for port in ports:
            if port == ACROSS:
                act(gather_copy(tile, side, port))
            else:
                @pl.when(has_next(port))
                def _():
                    act(gather_copy(tile, side, port))
        act(gather_pair(tile, side))

    def arrived(tile, side):
        gather_copy(tile, side, ACROSS).wait_recv()

    def start(copy):
        copy.start()

    def finish(copy):
        copy.wait_send()

    def relay_b(step, act):
        for port in (UP, DOWN):
            place = behind(port, step)

            @pl.when(inside(place))
            def _():
                tile = 2 * place + x
                if act is start:
                    arrived(tile, COMB)
                relay(tile, COMB, (port, ACROSS), act)

    def relay_a(step, act, own, part):
        for port in (UP, DOWN):
            place = behind(port, step)

            @pl.when(inside(place))
            def _():
                tile = 2 * place + (x if own else 1 - x)
                if act is start:
                    arrived(tile, part)
                relay(tile, part, (port,), act)

    def relay_a_across(act, part):
        if act is start:
            arrived(across, part)
        relay(across, part, (UP, DOWN), act)

    def relay_bx(step, act):
        for port in (UP, DOWN) if step else (UP,):
            place = behind(port, step)

            @pl.when(inside(place))
            def _():
                tile = 2 * place + 1 - x
                if act is start:
                    arrived(tile, COMB)
                relay(tile, COMB, (), act)

    def forward(tile, side):
        @pl.when(tile != chip)
        def _():
            gather_pair(tile, side).wait_recv()

        acc(side)[...] += product(halves(g_v[tile]), halves(gath(tile, side)[...]))

    def forward_step(step, kinds):
        def both(port, carry):
            place = behind(port, step)

            @pl.when(inside(place))
            def _():
                for side, own in kinds:
                    forward(2 * place + (x if own else 1 - x), side)

            return carry

        lax.fori_loop(0, 2 if step else 1, both, 0)

    def term_copy(tile):
        return pltpu.make_async_remote_copy(
            terms.at[tile, mate],
            other.at[tile],
            term_sems.at[0, tile],
            term_sems.at[1, tile],
            device_id=(2 * chip + mate, col),
            device_id_type=MESH,
        )

    def xone_copy(place, tile):
        return pltpu.make_async_remote_copy(
            terms.at[tile, core, pl.ds(PAIRED, lane - PAIRED)],
            xin_one.at[place],
            xone_sems.at[0, place],
            xone_sems.at[1, place],
            device_id=(2 * across + core, col),
            device_id_type=MESH,
        )

    def make_terms(count):
        tile = order(count)
        load_g(tile).wait()
        for part in (0, 1):
            rows = slice(part * half, (part + 1) * half)
            value = product((p_high[rows, :], p_low[rows, :]), halves(g_v[tile]))
            terms[tile, part] = value
        term_copy(tile).start()

    def pair_terms(count):
        tile = order(count)
        term_copy(tile).wait_recv()
        terms[tile, core] = terms[tile, core] + other[tile]

        @pl.when(count == 0)
        def _():
            xone_copy(tile // 2, tile).start()

    def send_across(count):
        tile = order(count)
        xone_copy(tile // 2, tile).start()

    def pieces(part, sub):
        size = (lane - PAIRED if part else PAIRED) // SUBS
        start = sub * size if isinstance(sub, int) else pl.multiple_of(sub * size, 8)
        return pl.ds(start, size), pl.ds(start + part * PAIRED, size)

    def pair_copy(port, step, slot, tile, sub):
        rows, _ = pieces(0, sub)
        return pltpu.make_async_remote_copy(
            terms.at[tile, core, rows],
            zin_pair.at[port, step - 1, slot, rows],
            pair_send.at[port, step - 1, slot, sub],
            pair_recv.at[port, step - 1, slot, sub],
            device_id=(2 * port_chip(port) + core, col),
            device_id_type=MESH,
        )

    def one_copy(port, step, tile, sub):
        rows, held = pieces(1, sub)
        return pltpu.make_async_remote_copy(
            terms.at[tile, core, held],
            zin_one.at[port, step - 1, rows],
            one_send.at[port, step - 1, sub],
            one_recv.at[port, step - 1, sub],
            device_id=(2 * port_chip(port) + core, col),
            device_id_type=MESH,
        )

    def sum_pair(step):
        for slot in (0, 1):
            for port in (UP, DOWN):
                place = ahead(port, step)

                @pl.when(inside(place))
                def _():
                    tile = 2 * place + (x if slot else 1 - x)

                    def each(sub, carry):
                        rows, _ = pieces(0, sub)
                        if step < nz - 1:
                            @pl.when(has_prev(port))
                            def _():
                                pair_copy(port, step + 1, slot, tile, sub).wait_recv()
                                terms[tile, core, rows] = (
                                    terms[tile, core, rows] + zin_pair[port, step, slot, rows]
                                )

                        pair_copy(port, step, slot, tile, sub).start()
                        return carry

                    lax.fori_loop(0, SUBS, each, 0)

    def sum_one(step):
        for port in (UP, DOWN):
            place = ahead(port, step)

            @pl.when(inside(place))
            def _():
                tile = 2 * place + x
                xone_copy(place, tile).wait_recv()

                def each(sub, carry):
                    rows, held = pieces(1, sub)
                    value = terms[tile, core, held] + xin_one[place, rows]
                    terms[tile, core, held] = value
                    if step < nz - 1:
                        @pl.when(has_prev(port))
                        def _():
                            one_copy(port, step + 1, tile, sub).wait_recv()
                            terms[tile, core, held] = value + zin_one[port, step, rows]

                    one_copy(port, step, tile, sub).start()
                    return carry

                lax.fori_loop(0, SUBS, each, 0)

    def last_copy(sub):
        rows, _ = pieces(0, sub)
        return pltpu.make_async_remote_copy(
            terms.at[across, core, rows],
            xin_last.at[rows],
            last_sems.at[0, sub],
            last_sems.at[1, sub],
            device_id=(2 * across + core, col),
            device_id_type=MESH,
        )

    def end_copy(part, plane, source_core, sub):
        _, held = pieces(part, sub)
        return pltpu.make_async_remote_copy(
            terms.at[chip, source_core, held],
            final.at[source_core, held],
            end_send.at[part, plane, sub],
            end_recv.at[part, source_core, sub],
            device_id=(2 * chip + col, col if plane == 0 else 1 - col),
            device_id_type=MESH,
        )

    def end_local(part, source_core, sub):
        _, held = pieces(part, sub)
        return pltpu.make_async_copy(
            terms.at[chip, source_core, held],
            final.at[source_core, held],
            end_recv.at[part, source_core, sub],
        )

    def give_end(part, sub):
        end_copy(part, 1, core, sub).start()

        @pl.when(core == col)
        def _():
            end_local(part, core, sub).start()

        @pl.when(core != col)
        def _():
            end_copy(part, 0, core, sub).start()

    def last_pair(sub, carry):
        rows, _ = pieces(0, sub)
        for slot in (0, 1):
            tile = chip if slot else across
            for port in (UP, DOWN):
                @pl.when(has_prev(port))
                def _():
                    pair_copy(port, 1, slot, tile, sub).wait_recv()
                    terms[tile, core, rows] = terms[tile, core, rows] + zin_pair[port, 0, slot, rows]

            if slot == 0:
                last_copy(sub).start()

        @pl.when(sub > 0)
        def _():
            last_across(sub - 1, carry)

        return carry

    def last_across(sub, carry):
        rows, _ = pieces(0, sub)
        last_copy(sub).wait_recv()
        terms[chip, core, rows] = terms[chip, core, rows] + xin_last[rows]
        give_end(0, sub)
        return carry

    def last_one(sub, carry):
        rows, held = pieces(1, sub)
        terms[chip, core, held] = terms[chip, core, held] + xin_one[z, rows]
        for port in (UP, DOWN):
            @pl.when(has_prev(port))
            def _():
                one_copy(port, 1, chip, sub).wait_recv()
                terms[chip, core, held] = terms[chip, core, held] + zin_one[port, 0, rows]

        give_end(1, sub)
        return carry

    def drain_early():
        own_first(finish)
        own_across(finish)
        own_along(finish)
        relay_a_across(finish, EARLY)
        relay_a_across(finish, LATE)
        relay_bx(0, finish)

        def drain_terms(count, carry):
            tile = order(count)
            term_copy(tile).wait_send()

            @pl.when(tile % 2 != x)
            def _():
                xone_copy(tile // 2, tile).wait_send()

            return carry

        lax.fori_loop(0, chips, drain_terms, 0)
        for step in range(1, nz):
            relay_b(step, finish)
            for part in (EARLY, LATE):
                relay_a(step, finish, True, part)
                relay_a(step, finish, False, part)
            relay_bx(step, finish)

    def drain_step(step):
        def both(port, carry):
            place = ahead(port, step)

            @pl.when(inside(place))
            def _():
                def each(sub, carry):
                    for slot in (0, 1):
                        pair_copy(port, step, slot, 2 * place + (x if slot else 1 - x), sub).wait_send()
                    one_copy(port, step, 2 * place + x, sub).wait_send()
                    return carry

                lax.fori_loop(0, SUBS, each, 0)

            return carry

        lax.fori_loop(0, 2, both, 0)

    def acc_copy(side):
        return pltpu.make_async_remote_copy(
            acc(side),
            acc_other(side),
            acc_sems.at[0, side],
            acc_sems.at[1, side],
            device_id=(2 * chip + core, 1 - col),
            device_id_type=MESH,
        )

    side_columns = pl.ds(pl.multiple_of(col * half, half), half)
    short = width // (2 * chips)

    def mate_copy(panel):
        return pltpu.make_async_remote_copy(
            diag_v.at[panel, :, mate],
            diag_mate.at[panel],
            mate_sems.at[0, panel],
            mate_sems.at[1, panel],
            device_id=(2 * chip + mate, col),
            device_id_type=MESH,
        )

    def part_copy(panel, source, target):
        return pltpu.make_async_remote_copy(
            diag_v.at[panel, target, core],
            diag_parts.at[panel, source],
            part_send.at[panel, target],
            part_recv.at[panel, source],
            device_id=(2 * target + core, col),
            device_id_type=MESH,
        )

    def swap_copy(panel):
        return pltpu.make_async_remote_copy(
            diag_out.at[panel, :, side_columns],
            diag_out.at[panel, :, side_columns],
            swap_sems.at[0, panel],
            swap_sems.at[1, panel],
            device_id=(2 * chip + core, 1 - col),
            device_id_type=MESH,
        )

    def adjoint_out(panel):
        columns = slice(panel * width, (panel + 1) * width)
        return pltpu.make_async_copy(adj_v.at[:, columns], adjoint.at[:, columns], out_sems.at[panel])

    def solve_first():
        for side in (EARLY, COMB, LATE):
            acc_copy(side).wait_recv()
            columns = columns_of(side)
            cot_t[0, :, columns] = adj_v[:, columns] - 2.0 * (acc(side)[...] + acc_other(side)[...])
        turned = product(halves(cot_t[0]), halves(inv_v[0]))
        adj_v[:, :width] = turned
        adjoint_out(0).start()
        cot_t[0] = turned.T

    def solve_second():
        for part in (0, 1):
            for source in (0, 1):
                for sub in range(SUBS):
                    end_local(part, source, sub).wait()
        coupled = final[...].reshape(width, width)
        cot_t[1] = product(halves(inv_v[1]), halves(cot_t[1] - 2.0 * coupled))

    def turn_cot():
        cot_t[1] = adj_v[:, width:].T

    def turn_inv():
        inv_v[1] = inv_v[1].T

    def diagonal(panel):
        place = pl.multiple_of(panel * width + col * half, half)
        own = p_v[:, pl.ds(place, half)]
        value = -product(halves(cot_t[panel]), halves(own))
        diag_v[panel] = value.reshape(chips, 2, short, half)
        mate_copy(panel).start()

    def give_second():
        adj_v[:, width:] = cot_t[1].T
        adjoint_out(1).start()

    def scatter(panel):
        mate_copy(panel).wait_recv()
        diag_v[panel, :, core] = diag_v[panel, :, core] + diag_mate[panel]
        for hop in range(1, chips):
            part_copy(panel, chip, (chip + hop) % chips).start()

    def collect(panel):
        total = diag_v[panel, chip, core]
        for hop in range(1, chips):
            source = (chip + hop) % chips
            part_copy(panel, source, chip).wait_recv()
            total = total + diag_parts[panel, source]
        diag_out[panel, :, side_columns] = total
        swap_copy(panel).start()

    @pl.when(core == col)
    def _():
        for side in (EARLY, COMB, LATE):
            load_own(side).wait()

    own_first(start)
    load_p(1).wait()
    for part in (0, 1):
        rows = slice(part * half, (part + 1) * half)
        high, low = halves(p_v[:, width + part * half:width + (part + 1) * half].T)
        p_high[rows, :] = high
        p_low[rows, :] = low
    acc_spine[...] = jnp.zeros_like(acc_spine)
    acc_comb[...] = jnp.zeros_like(acc_comb)
    chores = {
        3: lambda: (relay_a_across(start, EARLY),)[-1],
        7: lambda: (relay_a(1, start, True, EARLY), relay_b(1, start),)[-1],
    }

    def produce(count, carry):
        make_terms(count)
        pl.when(count > 0)(lambda: pair_terms(count - 1))
        for at, chore in chores.items():
            pl.when(count == at)(chore)
        return carry

    lax.fori_loop(0, chips, produce, 0)
    pair_terms(jnp.int32(chips - 1))

    own_across(start)
    relay_a(1, start, False, EARLY)
    sum_pair(3)
    relay_b(2, start)
    relay_bx(0, start)
    sum_pair(2)
    forward_step(1, [(EARLY, False)])
    relay_a(2, start, True, EARLY)
    send_across(2)
    forward_step(0, [(COMB, True)])
    relay_a(2, start, False, EARLY)
    forward_step(1, [(EARLY, True)])
    forward_step(0, [(COMB, False)])
    forward_step(2, [(EARLY, False), (COMB, True), (EARLY, True)])
    forward_step(0, [(EARLY, False)])
    relay_a_across(start, LATE)
    forward_step(0, [(EARLY, True)])
    relay_b(3, start)
    forward_step(3, [(COMB, True)])
    relay_a(3, start, True, EARLY)
    own_along(start)
    sum_one(3)
    forward_step(3, [(EARLY, True)])
    relay_bx(2, start)
    relay_bx(1, start)
    send_across(6)
    relay_a(3, start, False, EARLY)
    forward_step(3, [(EARLY, False)])
    relay_a(1, start, False, LATE)
    forward_step(1, [(COMB, True)])
    acc_copy(EARLY).start()
    relay_a(1, start, True, LATE)
    forward_step(0, [(LATE, False)])
    forward_step(2, [(COMB, False)])
    forward_step(1, [(COMB, False)])
    sum_one(2)
    relay_bx(3, start)
    forward_step(3, [(COMB, False)])
    acc_copy(COMB).start()
    relay_a(2, start, True, LATE)
    relay_a(2, start, False, LATE)
    forward_step(1, [(LATE, True)])
    send_across(4)
    sum_pair(1)
    forward_step(0, [(LATE, True)])
    forward_step(2, [(LATE, False)])
    relay_a(3, start, True, LATE)
    relay_a(3, start, False, LATE)
    forward_step(3, [(LATE, True)])
    forward_step(2, [(LATE, True)])
    forward_step(3, [(LATE, False)])
    forward_step(1, [(LATE, False)])
    acc_copy(LATE).start()
    sum_one(1)
    load_p(0).wait()
    load_cot.wait()
    load_inv.wait()
    turn_cot()
    turn_inv()
    drain_early()
    drain_step(3)
    drain_step(2)
    lax.fori_loop(0, SUBS, last_pair, 0)
    last_across(SUBS - 1, 0)
    xone_copy(z, chip).wait_recv()
    lax.fori_loop(0, SUBS, last_one, 0)
    solve_first()
    diagonal(0)
    scatter(0)
    drain_step(1)
    for sub in range(SUBS):
        last_copy(sub).wait_send()
    for side in (EARLY, COMB, LATE):
        acc_copy(side).wait_send()
    solve_second()
    diagonal(1)
    collect(0)
    scatter(1)
    give_second()
    collect(1)

    for sub in range(SUBS):
        for part in (0, 1):
            end_copy(part, 1, core, sub).wait_send()

            @pl.when(core != col)
            def _():
                end_copy(part, 0, core, sub).wait_send()

    for panel in (0, 1):
        mate_copy(panel).wait_send()
        for hop in range(1, chips):
            part_copy(panel, chip, (chip + hop) % chips).wait_send()
        swap_copy(panel).wait()
        adjoint_out(panel).wait()
    store = pltpu.make_async_copy(diag_out, diag, out_sems.at[2])
    store.start()
    store.wait()


def ladder_device(gbar, panels, panel_cot, inverses):
    width = inverses.shape[-1]
    chips = lax.axis_size("row") // 2
    nz = chips // 2
    half = width // 2
    short = width // (2 * chips)
    f32, bf16, dma = jnp.float32, jnp.bfloat16, pltpu.SemaphoreType.DMA
    anywhere = pl.BlockSpec(memory_space=pl.ANY)

    def kernel(*refs):
        ladder_kernel(nz, *refs)

    return pl.pallas_call(
        kernel,
        out_shape=(
            jax.ShapeDtypeStruct(panels.shape, f32),
            jax.ShapeDtypeStruct((2, short, width), f32),
        ),
        in_specs=[anywhere] * 4,
        out_specs=(anywhere, anywhere),
        scratch_shapes=[
            pltpu.VMEM((chips, width, width), f32),
            pltpu.VMEM(panels.shape, f32),
            pltpu.VMEM((2, chips, width, width // 4), f32),
            pltpu.VMEM((chips, width, half), f32),
            pltpu.VMEM((chips, 2, half, width), f32),
            pltpu.VMEM((chips, half, width), f32),
            pltpu.VMEM((2, nz - 1, 2, PAIRED, width), f32),
            pltpu.VMEM((2, nz - 1, half - PAIRED, width), f32),
            pltpu.VMEM((nz, half - PAIRED, width), f32),
            pltpu.VMEM((PAIRED, width), f32),
            pltpu.VMEM((2, half, width), f32),
            pltpu.VMEM((2, width, width // 4), f32),
            pltpu.VMEM((width, half), f32),
            pltpu.VMEM((2, width, width // 4), f32),
            pltpu.VMEM((width, half), f32),
            pltpu.VMEM((width, width), bf16),
            pltpu.VMEM((width, width), bf16),
            pltpu.VMEM(inverses.shape, f32),
            pltpu.VMEM(inverses.shape, f32),
            pltpu.VMEM(panels.shape, f32),
            pltpu.VMEM((2, chips, 2, short, half), f32),
            pltpu.VMEM((2, chips, short, half), f32),
            pltpu.VMEM((2, chips, short, half), f32),
            pltpu.VMEM((2, short, width), f32),
            dma((chips + 4,)),
            dma((3,)),
            dma((3,)),
            dma((3, chips, 3)),
            dma((chips, 3)),
            dma((2, chips, 3)),
            dma((2, chips)),
            dma((2, nz)),
            dma((2, nz - 1, 2, SUBS)),
            dma((2, nz - 1, 2, SUBS)),
            dma((2, nz - 1, SUBS)),
            dma((2, nz - 1, SUBS)),
            dma((2, SUBS)),
            dma((2, 2, SUBS)),
            dma((2, 2, SUBS)),
            dma((2, 3)),
            dma((2, 2)),
            dma((2, chips)),
            dma((2, chips)),
            dma((2, 2)),
        ],
        compiler_params=pltpu.CompilerParams(
            collective_id=0, has_side_effects=True, vmem_limit_bytes=62 * 1024 * 1024
        ),
    )(gbar, panels, panel_cot, inverses)


def plain_device(gbar, panels, panel_cot, inverses):
    width = inverses.shape[-1]
    mode = lax.Precision.HIGHEST
    row_id = lax.axis_index("row")
    col_count = lax.axis_size("col")
    contract = (((0,), (0,)), ((), ()))
    partial_value = lax.dot_general(
        gbar, panels, contract, precision=mode, preferred_element_type=jnp.float32
    )
    summed = lax.psum(partial_value, "row")
    own_tile = lax.dynamic_slice_in_dim(summed, row_id // col_count * width, width, 0)
    own_tile = jnp.where(lax.axis_index("col") == row_id % col_count, own_tile, 0)
    combined = panel_cot - 2.0 * lax.psum(own_tile, "col")
    adjoint, terms = [], []
    for panel in (0, 1):
        columns = slice(panel * width, (panel + 1) * width)
        adjoint.append(
            jnp.dot(combined[:, columns], inverses[panel], precision=mode, preferred_element_type=jnp.float32)
        )
        terms.append(
            -lax.dot_general(
                adjoint[-1], panels[:, columns], contract, precision=mode, preferred_element_type=jnp.float32
            )
        )
    diag_adjoint = lax.psum_scatter(jnp.stack(terms), "row", scatter_dimension=1, tiled=True)
    return jnp.concatenate(adjoint, axis=1), diag_adjoint


def solution(mesh):
    in_specs = (P("row", "col"), P("row", None), P("row", None), P())
    out_specs = (P("row", None), P(None, "row", None))
    on_ladder = mesh.shape["col"] == 2 and mesh.shape["row"] == 16
    return jax.shard_map(
        ladder_device if on_ladder else plain_device,
        mesh=mesh, in_specs=in_specs, out_specs=out_specs, check_vma=False,
    )
```

```python
import jax
import jax.numpy as jnp
from jax import lax
from jax.experimental import pallas as pl
from jax.experimental.pallas import tpu as pltpu
from jax.sharding import PartitionSpec as P

MESH = pl.DeviceIdType.MESH
SUBS = 4
UP, DOWN, ACROSS = 0, 1, 2
EARLY, COMB, LATE = 0, 1, 2
PAIRED = 96


def halves(value):
    high = value.astype(jnp.bfloat16)
    low = (value - high.astype(jnp.float32)).astype(jnp.bfloat16)
    return high, low


def product(left, right):
    (left_high, left_low), (right_high, right_low) = left, right

    def one(a, b):
        return jnp.dot(a, b, preferred_element_type=jnp.float32)

    return one(left_high, right_low) + one(left_low, right_high) + one(left_high, right_high)


def ladder_kernel(
    nz, gbar, panels, cot, inverses,
    adjoint, diag,
    g_v, p_v, gath_spine, gath_comb, terms, other, zin_pair, zin_one, xin_one, xin_last, final,
    acc_spine, acc_comb, acc_spine_other, acc_comb_other, p_high, p_low, inv_v, cot_t, adj_t, adj_v,
    diag_v, diag_mate, diag_parts, diag_out,
    load_sems, own_sems, out_sems,
    gath_send, gath_recv, gath_mate,
    term_sems, xone_sems, pair_send, pair_recv, one_send, one_recv, last_sems,
    end_send, end_recv, acc_sems,
    mate_sems, part_send, part_recv, swap_sems,
):
    width = inverses.shape[-1]
    chips = 2 * nz
    half = width // 2
    lane = half
    split = width - 2 * PAIRED
    row = lax.axis_index("row")
    col = lax.axis_index("col")
    chip = row // 2
    core = row % 2
    mate = 1 - core
    x = chip % 2
    z = chip // 2
    across = 2 * z + 1 - x

    def port_chip(port):
        if isinstance(port, int) and port == ACROSS:
            return across
        return chip + 2 - 4 * port

    def has_next(port):
        return jnp.where(port == UP, z < nz - 1, z > 0)

    def has_prev(port):
        return jnp.where(port == UP, z > 0, z < nz - 1)

    def behind(port, step):
        return z - step + 2 * step * port

    def ahead(port, step):
        return z + step - 2 * step * port

    def inside(place):
        return (place >= 0) & (place < nz)

    def load_g(tile):
        start = pl.multiple_of(tile * width, width)
        return pltpu.make_async_copy(gbar.at[:, pl.ds(start, width)], g_v.at[tile], load_sems.at[tile])

    def load_p(panel):
        columns = slice(panel * width, (panel + 1) * width)
        return pltpu.make_async_copy(panels.at[:, columns], p_v.at[:, columns], load_sems.at[chips + panel])

    def columns_of(side):
        quarter = width // 4
        return {EARLY: slice(0, quarter), LATE: slice(quarter, half), COMB: slice(half, width)}[side]

    def gath(tile, side):
        return gath_comb.at[tile] if side == COMB else gath_spine.at[side // 2, tile]

    def acc(side):
        return acc_comb if side == COMB else acc_spine.at[side // 2]

    def acc_other(side):
        return acc_comb_other if side == COMB else acc_spine_other.at[side // 2]

    def load_own(side):
        return pltpu.make_async_copy(panels.at[:, columns_of(side)], gath(chip, side), own_sems.at[side])

    load_cot = pltpu.make_async_copy(cot, adj_v, load_sems.at[chips + 2])
    load_inv = pltpu.make_async_copy(inverses, inv_v, load_sems.at[chips + 3])

    def order(count):
        place = jnp.where(z < nz // 2, nz - 1 - count // 2, count // 2)
        return 2 * place + jnp.where(count % 2 == 0, 1 - x, x)

    @pl.when(core == col)
    def _():
        for side in (EARLY, COMB, LATE):
            load_own(side).start()

    load_p(1).start()
    for count in range(chips):
        load_g(order(count)).start()
    load_p(0).start()
    load_cot.start()
    load_inv.start()

    barrier = pltpu.get_barrier_semaphore()
    friends = [
        (2 * across + core, col),
        (2 * chip + mate, col),
        (2 * chip + core, 1 - col),
        (2 * chip + mate, 1 - col),
    ]

    def greet(friend):
        pl.semaphore_signal(barrier, inc=1, device_id=friend, device_id_type=MESH)

    for friend in friends:
        greet(friend)
    for port in (UP, DOWN):
        pl.when(has_next(port))(lambda: greet((2 * port_chip(port) + core, col)))

    pl.semaphore_wait(barrier, len(friends) + jnp.where((z > 0) & (z < nz - 1), 2, 1))

    def gather_copy(tile, side, port):
        rows = pl.ds(pl.multiple_of(core * half, half), half)
        return pltpu.make_async_remote_copy(
            gath(tile, side).at[rows],
            gath(tile, side).at[rows],
            gath_send.at[port, tile, side],
            gath_recv.at[tile, side],
            device_id=(2 * port_chip(port) + core, col),
            device_id_type=MESH,
        )

    def gather_pair(tile, side):
        rows = pl.ds(pl.multiple_of(core * half, half), half)
        return pltpu.make_async_remote_copy(
            gath(tile, side).at[rows],
            gath(tile, side).at[rows],
            gath_mate.at[0, tile, side],
            gath_mate.at[1, tile, side],
            device_id=(2 * chip + mate, col),
            device_id_type=MESH,
        )

    def gather_own_pair(side):
        return pltpu.make_async_remote_copy(
            gath(chip, side),
            gath(chip, side),
            gath_mate.at[0, chip, side],
            gath_mate.at[1, chip, side],
            device_id=(2 * chip + mate, col),
            device_id_type=MESH,
        )

    def own_sends(act, routes, sides):
        @pl.when(core == col)
        def _():
            for side in sides:
                act(gather_own_pair(side))

        for side, port in routes:
            if side in sides and act is start:
                @pl.when(core != col)
                def _():
                    gather_own_pair(side).wait_recv()

                sides = tuple(other for other in sides if other != side)
            copy = gather_copy(chip, side, port)
            if port == ACROSS:
                act(copy)
            else:
                pl.when(has_next(port))(lambda: act(copy))

    first_routes = [(EARLY, ACROSS), (COMB, UP), (COMB, DOWN), (EARLY, UP), (EARLY, DOWN), (COMB, ACROSS)]

    def own_first(act):
        own_sends(act, first_routes, (EARLY, COMB))

    def own_across(act):
        own_sends(act, [(LATE, ACROSS)], (LATE,))

    def own_along(act):
        own_sends(act, [(LATE, UP), (LATE, DOWN)], ())

    def relay(tile, side, ports, act):
        for port in ports:
            if port == ACROSS:
                act(gather_copy(tile, side, port))
            else:
                @pl.when(has_next(port))
                def _():
                    act(gather_copy(tile, side, port))
        act(gather_pair(tile, side))

    def arrived(tile, side):
        gather_copy(tile, side, ACROSS).wait_recv()

    def start(copy):
        copy.start()

    def finish(copy):
        copy.wait_send()

    def relay_b(step, act):
        for port in (UP, DOWN):
            place = behind(port, step)

            @pl.when(inside(place))
            def _():
                tile = 2 * place + x
                if act is start:
                    arrived(tile, COMB)
                relay(tile, COMB, (port, ACROSS), act)

    def relay_a(step, act, own, part):
        for port in (UP, DOWN):
            place = behind(port, step)

            @pl.when(inside(place))
            def _():
                tile = 2 * place + (x if own else 1 - x)
                if act is start:
                    arrived(tile, part)
                relay(tile, part, (port,), act)

    def relay_a_across(act, part):
        if act is start:
            arrived(across, part)
        relay(across, part, (UP, DOWN), act)

    def relay_bx(step, act):
        for port in (UP, DOWN) if step else (UP,):
            place = behind(port, step)

            @pl.when(inside(place))
            def _():
                tile = 2 * place + 1 - x
                if act is start:
                    arrived(tile, COMB)
                relay(tile, COMB, (), act)

    def forward(tile, side):
        @pl.when(tile != chip)
        def _():
            gather_pair(tile, side).wait_recv()

        acc(side)[...] += product(halves(g_v[tile]), halves(gath(tile, side)[...]))

    def forward_step(step, kinds):
        def both(port, carry):
            place = behind(port, step)

            @pl.when(inside(place))
            def _():
                for side, own in kinds:
                    forward(2 * place + (x if own else 1 - x), side)

            return carry

        lax.fori_loop(0, 2 if step else 1, both, 0)

    def term_copy(tile):
        return pltpu.make_async_remote_copy(
            terms.at[tile, mate],
            other.at[tile],
            term_sems.at[0, tile],
            term_sems.at[1, tile],
            device_id=(2 * chip + mate, col),
            device_id_type=MESH,
        )

    def xone_copy(place, tile):
        return pltpu.make_async_remote_copy(
            terms.at[tile, core, pl.ds(PAIRED, lane - PAIRED)],
            xin_one.at[place],
            xone_sems.at[0, place],
            xone_sems.at[1, place],
            device_id=(2 * across + core, col),
            device_id_type=MESH,
        )

    def make_terms(count):
        tile = order(count)
        load_g(tile).wait()
        for part in (0, 1):
            rows = slice(part * half, (part + 1) * half)
            value = product((p_high[rows, :], p_low[rows, :]), halves(g_v[tile]))
            terms[tile, part] = value
        term_copy(tile).start()

    def pair_terms(count):
        tile = order(count)
        term_copy(tile).wait_recv()
        terms[tile, core] = terms[tile, core] + other[tile]

        @pl.when(count == 0)
        def _():
            xone_copy(tile // 2, tile).start()

    def send_across(count):
        tile = order(count)
        xone_copy(tile // 2, tile).start()

    def pieces(part, sub):
        size = (lane - PAIRED if part else PAIRED) // SUBS
        start = sub * size if isinstance(sub, int) else pl.multiple_of(sub * size, 8)
        return pl.ds(start, size), pl.ds(start + part * PAIRED, size)

    def pair_copy(port, step, slot, tile, sub):
        rows, _ = pieces(0, sub)
        return pltpu.make_async_remote_copy(
            terms.at[tile, core, rows],
            zin_pair.at[port, step - 1, slot, rows],
            pair_send.at[port, step - 1, slot, sub],
            pair_recv.at[port, step - 1, slot, sub],
            device_id=(2 * port_chip(port) + core, col),
            device_id_type=MESH,
        )

    def one_copy(port, step, tile, sub):
        rows, held = pieces(1, sub)
        return pltpu.make_async_remote_copy(
            terms.at[tile, core, held],
            zin_one.at[port, step - 1, rows],
            one_send.at[port, step - 1, sub],
            one_recv.at[port, step - 1, sub],
            device_id=(2 * port_chip(port) + core, col),
            device_id_type=MESH,
        )

    def sum_pair(step):
        for slot in (0, 1):
            for port in (UP, DOWN):
                place = ahead(port, step)

                @pl.when(inside(place))
                def _():
                    tile = 2 * place + (x if slot else 1 - x)

                    def each(sub, carry):
                        rows, _ = pieces(0, sub)
                        if step < nz - 1:
                            @pl.when(has_prev(port))
                            def _():
                                pair_copy(port, step + 1, slot, tile, sub).wait_recv()
                                terms[tile, core, rows] = (
                                    terms[tile, core, rows] + zin_pair[port, step, slot, rows]
                                )

                        pair_copy(port, step, slot, tile, sub).start()
                        return carry

                    lax.fori_loop(0, SUBS, each, 0)

    def sum_one(step):
        for port in (UP, DOWN):
            place = ahead(port, step)

            @pl.when(inside(place))
            def _():
                tile = 2 * place + x
                xone_copy(place, tile).wait_recv()

                def each(sub, carry):
                    rows, held = pieces(1, sub)
                    value = terms[tile, core, held] + xin_one[place, rows]
                    terms[tile, core, held] = value
                    if step < nz - 1:
                        @pl.when(has_prev(port))
                        def _():
                            one_copy(port, step + 1, tile, sub).wait_recv()
                            terms[tile, core, held] = value + zin_one[port, step, rows]

                    one_copy(port, step, tile, sub).start()
                    return carry

                lax.fori_loop(0, SUBS, each, 0)

    def last_copy(sub):
        rows, _ = pieces(0, sub)
        return pltpu.make_async_remote_copy(
            terms.at[across, core, rows],
            xin_last.at[rows],
            last_sems.at[0, sub],
            last_sems.at[1, sub],
            device_id=(2 * across + core, col),
            device_id_type=MESH,
        )

    def final_rows(part, source_core, sub):
        size = lane - PAIRED if part else PAIRED
        start = source_core * size + sub * (size // SUBS) + (0 if part else split)
        return pl.ds(start if isinstance(start, int) else pl.multiple_of(start, 8), size // SUBS)

    def end_copy(part, plane, source_core, sub):
        _, held = pieces(part, sub)
        return pltpu.make_async_remote_copy(
            terms.at[chip, source_core, held],
            final.at[final_rows(part, source_core, sub)],
            end_send.at[part, plane, sub],
            end_recv.at[part, source_core, sub],
            device_id=(2 * chip + col, col if plane == 0 else 1 - col),
            device_id_type=MESH,
        )

    def end_local(part, source_core, sub):
        _, held = pieces(part, sub)
        return pltpu.make_async_copy(
            terms.at[chip, source_core, held],
            final.at[final_rows(part, source_core, sub)],
            end_recv.at[part, source_core, sub],
        )

    def give_end(part, sub):
        end_copy(part, 1, core, sub).start()

        @pl.when(core == col)
        def _():
            end_local(part, core, sub).start()

        @pl.when(core != col)
        def _():
            end_copy(part, 0, core, sub).start()

    def last_pair(sub, carry):
        rows, _ = pieces(0, sub)
        for slot in (0, 1):
            tile = chip if slot else across
            for port in (UP, DOWN):
                @pl.when(has_prev(port))
                def _():
                    pair_copy(port, 1, slot, tile, sub).wait_recv()
                    terms[tile, core, rows] = terms[tile, core, rows] + zin_pair[port, 0, slot, rows]

            if slot == 0:
                last_copy(sub).start()

        @pl.when(sub > 0)
        def _():
            last_across(sub - 1, carry)

        return carry

    def last_across(sub, carry):
        rows, _ = pieces(0, sub)
        last_copy(sub).wait_recv()
        terms[chip, core, rows] = terms[chip, core, rows] + xin_last[rows]
        give_end(0, sub)
        return carry

    def last_one(sub, carry):
        rows, held = pieces(1, sub)
        terms[chip, core, held] = terms[chip, core, held] + xin_one[z, rows]
        for port in (UP, DOWN):
            @pl.when(has_prev(port))
            def _():
                one_copy(port, 1, chip, sub).wait_recv()
                terms[chip, core, held] = terms[chip, core, held] + zin_one[port, 0, rows]

        give_end(1, sub)
        return carry

    def drain_early():
        own_first(finish)
        own_across(finish)
        own_along(finish)
        relay_a_across(finish, EARLY)
        relay_a_across(finish, LATE)
        relay_bx(0, finish)

        def drain_terms(count, carry):
            tile = order(count)
            term_copy(tile).wait_send()

            @pl.when(tile % 2 != x)
            def _():
                xone_copy(tile // 2, tile).wait_send()

            return carry

        lax.fori_loop(0, chips, drain_terms, 0)
        for step in range(1, nz):
            relay_b(step, finish)
            for part in (EARLY, LATE):
                relay_a(step, finish, True, part)
                relay_a(step, finish, False, part)
            relay_bx(step, finish)

    def drain_step(step):
        def both(port, carry):
            place = ahead(port, step)

            @pl.when(inside(place))
            def _():
                def each(sub, carry):
                    for slot in (0, 1):
                        pair_copy(port, step, slot, 2 * place + (x if slot else 1 - x), sub).wait_send()
                    one_copy(port, step, 2 * place + x, sub).wait_send()
                    return carry

                lax.fori_loop(0, SUBS, each, 0)

            return carry

        lax.fori_loop(0, 2, both, 0)

    def acc_copy(side):
        return pltpu.make_async_remote_copy(
            acc(side),
            acc_other(side),
            acc_sems.at[0, side],
            acc_sems.at[1, side],
            device_id=(2 * chip + core, 1 - col),
            device_id_type=MESH,
        )

    side_columns = pl.ds(pl.multiple_of(col * half, half), half)
    short = width // (2 * chips)

    bound = split // (2 * short)
    groups = ((0, 0, chips), (1, bound, chips), (1, 0, bound))

    def mate_copy(group):
        panel, low, high = groups[group]
        return pltpu.make_async_remote_copy(
            diag_v.at[panel, low:high, mate],
            diag_mate.at[panel, low:high],
            mate_sems.at[0, group],
            mate_sems.at[1, group],
            device_id=(2 * chip + mate, col),
            device_id_type=MESH,
        )

    def part_copy(panel, source, target):
        return pltpu.make_async_remote_copy(
            diag_v.at[panel, target, core],
            diag_parts.at[panel, source],
            part_send.at[panel, target],
            part_recv.at[panel, source],
            device_id=(2 * target + core, col),
            device_id_type=MESH,
        )

    def swap_copy(panel):
        return pltpu.make_async_remote_copy(
            diag_out.at[panel, :, side_columns],
            diag_out.at[panel, :, side_columns],
            swap_sems.at[0, panel],
            swap_sems.at[1, panel],
            device_id=(2 * chip + core, 1 - col),
            device_id_type=MESH,
        )

    def adjoint_out(panel):
        columns = slice(panel * width, (panel + 1) * width)
        return pltpu.make_async_copy(adj_v.at[:, columns], adjoint.at[:, columns], out_sems.at[panel])

    def solve_first():
        for side in (EARLY, COMB, LATE):
            acc_copy(side).wait_recv()
            columns = columns_of(side)
            cot_t[0, :, columns] = adj_v[:, columns] - 2.0 * (acc(side)[...] + acc_other(side)[...])
        turned = product(halves(cot_t[0]), halves(inv_v[0]))
        adj_v[:, :width] = turned
        adjoint_out(0).start()
        cot_t[0] = turned.T

    def wait_end(part):
        for source in (0, 1):
            for sub in range(SUBS):
                end_local(part, source, sub).wait()

    def solve_high():
        wait_end(0)
        cot_t[1, split:] = cot_t[1, split:] - 2.0 * final[split:]
        first = split // 128 * 128
        adj_t[split:] = product(halves(inv_v[1, split:, first:]), halves(cot_t[1, first:]))

    def solve_low():
        wait_end(1)
        cot_t[1, :split] = cot_t[1, :split] - 2.0 * final[:split]
        adj_t[:split] = product(halves(inv_v[1, :split]), halves(cot_t[1]))

    def turn_cot():
        cot_t[1] = adj_v[:, width:].T

    def turn_inv():
        inv_v[1] = inv_v[1].T

    def diagonal(group):
        panel, low, high = groups[group]
        place = pl.multiple_of(panel * width + col * half, half)
        own = p_v[:, pl.ds(place, half)]
        source = adj_t[2 * short * low:2 * short * high] if panel else cot_t[0]
        value = -product(halves(source), halves(own))
        diag_v[panel, low:high] = value.reshape(high - low, 2, short, half)
        mate_copy(group).start()

    def give_second():
        adj_v[:, width:] = adj_t[...].T
        adjoint_out(1).start()

    def scatter(group):
        panel, low, high = groups[group]
        mate_copy(group).wait_recv()
        diag_v[panel, low:high, core] = diag_v[panel, low:high, core] + diag_mate[panel, low:high]
        for hop in range(1, chips):
            target = (chip + hop) % chips

            @pl.when((target >= low) & (target < high))
            def _():
                part_copy(panel, chip, target).start()

    def collect(panel):
        total = diag_v[panel, chip, core]
        for hop in range(1, chips):
            source = (chip + hop) % chips
            part_copy(panel, source, chip).wait_recv()
            total = total + diag_parts[panel, source]
        diag_out[panel, :, side_columns] = total
        swap_copy(panel).start()

    @pl.when(core == col)
    def _():
        for side in (EARLY, COMB, LATE):
            load_own(side).wait()

    own_first(start)
    load_p(1).wait()
    high, low = halves(p_v[:, width:].T)
    for part in (0, 1):
        for to, first, size in (
            (part * half, split + part * PAIRED, PAIRED),
            (part * half + PAIRED, part * (half - PAIRED), half - PAIRED),
        ):
            p_high[to:to + size, :] = high[first:first + size]
            p_low[to:to + size, :] = low[first:first + size]

    acc_spine[...] = jnp.zeros_like(acc_spine)
    acc_comb[...] = jnp.zeros_like(acc_comb)
    chores = {
        3: lambda: (relay_a_across(start, EARLY),)[-1],
        7: lambda: (relay_a(1, start, True, EARLY), relay_b(1, start),)[-1],
    }

    def produce(count, carry):
        make_terms(count)
        pl.when(count > 0)(lambda: pair_terms(count - 1))
        for at, chore in chores.items():
            pl.when(count == at)(chore)
        return carry

    lax.fori_loop(0, chips, produce, 0)
    pair_terms(jnp.int32(chips - 1))

    own_across(start)
    relay_a(1, start, False, EARLY)
    sum_pair(3)
    relay_b(2, start)
    relay_bx(0, start)
    sum_pair(2)
    forward_step(1, [(EARLY, False)])
    relay_a(2, start, True, EARLY)
    send_across(2)
    forward_step(0, [(COMB, True)])
    relay_a(2, start, False, EARLY)
    forward_step(1, [(EARLY, True)])
    forward_step(0, [(COMB, False)])
    forward_step(2, [(EARLY, False), (COMB, True), (EARLY, True)])
    forward_step(0, [(EARLY, False)])
    relay_a_across(start, LATE)
    forward_step(0, [(EARLY, True)])
    relay_b(3, start)
    forward_step(3, [(COMB, True)])
    relay_a(3, start, True, EARLY)
    own_along(start)
    sum_one(3)
    forward_step(3, [(EARLY, True)])
    relay_bx(2, start)
    relay_bx(1, start)
    send_across(6)
    relay_a(3, start, False, EARLY)
    forward_step(3, [(EARLY, False)])
    relay_a(1, start, False, LATE)
    forward_step(1, [(COMB, True)])
    acc_copy(EARLY).start()
    relay_a(1, start, True, LATE)
    forward_step(0, [(LATE, False)])
    forward_step(2, [(COMB, False)])
    forward_step(1, [(COMB, False)])
    sum_one(2)
    relay_bx(3, start)
    forward_step(3, [(COMB, False)])
    acc_copy(COMB).start()
    relay_a(2, start, True, LATE)
    relay_a(2, start, False, LATE)
    forward_step(1, [(LATE, True)])
    send_across(4)
    sum_pair(1)
    forward_step(0, [(LATE, True)])
    forward_step(2, [(LATE, False)])
    relay_a(3, start, True, LATE)
    relay_a(3, start, False, LATE)
    forward_step(3, [(LATE, True)])
    forward_step(2, [(LATE, True)])
    forward_step(3, [(LATE, False)])
    forward_step(1, [(LATE, False)])
    acc_copy(LATE).start()
    sum_one(1)
    load_p(0).wait()
    load_cot.wait()
    load_inv.wait()
    turn_cot()
    turn_inv()
    lax.fori_loop(0, SUBS, last_pair, 0)
    last_across(SUBS - 1, 0)
    solve_first()
    diagonal(0)
    xone_copy(z, chip).wait_recv()
    lax.fori_loop(0, SUBS, last_one, 0)
    scatter(0)
    solve_high()
    diagonal(1)
    scatter(1)
    solve_low()
    diagonal(2)
    scatter(2)
    drain_step(1)
    for sub in range(SUBS):
        last_copy(sub).wait_send()
    for side in (EARLY, COMB, LATE):
        acc_copy(side).wait_send()
    drain_early()
    drain_step(3)
    drain_step(2)
    collect(0)
    give_second()
    collect(1)

    for sub in range(SUBS):
        for part in (0, 1):
            end_copy(part, 1, core, sub).wait_send()

            @pl.when(core != col)
            def _():
                end_copy(part, 0, core, sub).wait_send()

    for group in range(len(groups)):
        mate_copy(group).wait_send()
    for panel in (0, 1):
        for hop in range(1, chips):
            part_copy(panel, chip, (chip + hop) % chips).wait_send()
        swap_copy(panel).wait()
        adjoint_out(panel).wait()
    store = pltpu.make_async_copy(diag_out, diag, out_sems.at[2])
    store.start()
    store.wait()


def ladder_device(gbar, panels, panel_cot, inverses):
    width = inverses.shape[-1]
    chips = lax.axis_size("row") // 2
    nz = chips // 2
    half = width // 2
    short = width // (2 * chips)
    f32, bf16, dma = jnp.float32, jnp.bfloat16, pltpu.SemaphoreType.DMA
    anywhere = pl.BlockSpec(memory_space=pl.ANY)

    def kernel(*refs):
        ladder_kernel(nz, *refs)

    return pl.pallas_call(
        kernel,
        out_shape=(
            jax.ShapeDtypeStruct(panels.shape, f32),
            jax.ShapeDtypeStruct((2, short, width), f32),
        ),
        in_specs=[anywhere] * 4,
        out_specs=(anywhere, anywhere),
        scratch_shapes=[
            pltpu.VMEM((chips, width, width), f32),
            pltpu.VMEM(panels.shape, f32),
            pltpu.VMEM((2, chips, width, width // 4), f32),
            pltpu.VMEM((chips, width, half), f32),
            pltpu.VMEM((chips, 2, half, width), f32),
            pltpu.VMEM((chips, half, width), f32),
            pltpu.VMEM((2, nz - 1, 2, PAIRED, width), f32),
            pltpu.VMEM((2, nz - 1, half - PAIRED, width), f32),
            pltpu.VMEM((nz, half - PAIRED, width), f32),
            pltpu.VMEM((PAIRED, width), f32),
            pltpu.VMEM((width, width), f32),
            pltpu.VMEM((2, width, width // 4), f32),
            pltpu.VMEM((width, half), f32),
            pltpu.VMEM((2, width, width // 4), f32),
            pltpu.VMEM((width, half), f32),
            pltpu.VMEM((width, width), bf16),
            pltpu.VMEM((width, width), bf16),
            pltpu.VMEM(inverses.shape, f32),
            pltpu.VMEM(inverses.shape, f32),
            pltpu.VMEM((width, width), f32),
            pltpu.VMEM(panels.shape, f32),
            pltpu.VMEM((2, chips, 2, short, half), f32),
            pltpu.VMEM((2, chips, short, half), f32),
            pltpu.VMEM((2, chips, short, half), f32),
            pltpu.VMEM((2, short, width), f32),
            dma((chips + 4,)),
            dma((3,)),
            dma((3,)),
            dma((3, chips, 3)),
            dma((chips, 3)),
            dma((2, chips, 3)),
            dma((2, chips)),
            dma((2, nz)),
            dma((2, nz - 1, 2, SUBS)),
            dma((2, nz - 1, 2, SUBS)),
            dma((2, nz - 1, SUBS)),
            dma((2, nz - 1, SUBS)),
            dma((2, SUBS)),
            dma((2, 2, SUBS)),
            dma((2, 2, SUBS)),
            dma((2, 3)),
            dma((2, 3)),
            dma((2, chips)),
            dma((2, chips)),
            dma((2, 2)),
        ],
        compiler_params=pltpu.CompilerParams(
            collective_id=0, has_side_effects=True, vmem_limit_bytes=62 * 1024 * 1024
        ),
    )(gbar, panels, panel_cot, inverses)


def plain_device(gbar, panels, panel_cot, inverses):
    width = inverses.shape[-1]
    mode = lax.Precision.HIGHEST
    row_id = lax.axis_index("row")
    col_count = lax.axis_size("col")
    contract = (((0,), (0,)), ((), ()))
    partial_value = lax.dot_general(
        gbar, panels, contract, precision=mode, preferred_element_type=jnp.float32
    )
    summed = lax.psum(partial_value, "row")
    own_tile = lax.dynamic_slice_in_dim(summed, row_id // col_count * width, width, 0)
    own_tile = jnp.where(lax.axis_index("col") == row_id % col_count, own_tile, 0)
    combined = panel_cot - 2.0 * lax.psum(own_tile, "col")
    adjoint, terms = [], []
    for panel in (0, 1):
        columns = slice(panel * width, (panel + 1) * width)
        adjoint.append(
            jnp.dot(combined[:, columns], inverses[panel], precision=mode, preferred_element_type=jnp.float32)
        )
        terms.append(
            -lax.dot_general(
                adjoint[-1], panels[:, columns], contract, precision=mode, preferred_element_type=jnp.float32
            )
        )
    diag_adjoint = lax.psum_scatter(jnp.stack(terms), "row", scatter_dimension=1, tiled=True)
    return jnp.concatenate(adjoint, axis=1), diag_adjoint


def solution(mesh):
    in_specs = (P("row", "col"), P("row", None), P("row", None), P())
    out_specs = (P("row", None), P(None, "row", None))
    on_ladder = mesh.shape["col"] == 2 and mesh.shape["row"] == 16
    return jax.shard_map(
        ladder_device if on_ladder else plain_device,
        mesh=mesh, in_specs=in_specs, out_specs=out_specs, check_vma=False,
    )
```

```python
import jax
import jax.numpy as jnp
from jax import lax
from jax.experimental import pallas as pl
from jax.experimental.pallas import tpu as pltpu
from jax.sharding import PartitionSpec as P

MESH = pl.DeviceIdType.MESH
SUBS = 2
UP, DOWN, ACROSS = 0, 1, 2
EARLY, COMB, LATE = 0, 1, 2
PAIRED = 96


def halves(value):
    high = value.astype(jnp.bfloat16)
    low = (value - high.astype(jnp.float32)).astype(jnp.bfloat16)
    return high, low


def product(left, right):
    (left_high, left_low), (right_high, right_low) = left, right

    def one(a, b):
        return jnp.dot(a, b, preferred_element_type=jnp.float32)

    return one(left_high, right_low) + one(left_low, right_high) + one(left_high, right_high)


def ladder_kernel(
    nz, gbar, panels, cot, inverses,
    adjoint, diag,
    g_v, p_v, gath_spine, gath_comb, terms, other, zin_pair, zin_one, xin_one, xin_last, final,
    acc_spine, acc_comb, acc_spine_other, acc_comb_other, p_high, p_low, inv_v, cot_t, adj_t, adj_v,
    diag_v, diag_mate, diag_parts, diag_out,
    load_sems, own_sems, out_sems,
    gath_send, gath_recv, gath_mate,
    term_sems, xone_sems, pair_send, pair_recv, one_send, one_recv, last_sems,
    end_send, end_recv, acc_sems,
    mate_sems, part_send, part_recv, swap_sems,
):
    width = inverses.shape[-1]
    chips = 2 * nz
    half = width // 2
    lane = half
    split = width - 2 * PAIRED
    row = lax.axis_index("row")
    col = lax.axis_index("col")
    chip = row // 2
    core = row % 2
    mate = 1 - core
    x = chip % 2
    z = chip // 2
    across = 2 * z + 1 - x

    def port_chip(port):
        if isinstance(port, int) and port == ACROSS:
            return across
        return chip + 2 - 4 * port

    def has_next(port):
        return jnp.where(port == UP, z < nz - 1, z > 0)

    def has_prev(port):
        return jnp.where(port == UP, z > 0, z < nz - 1)

    def behind(port, step):
        return z - step + 2 * step * port

    def ahead(port, step):
        return z + step - 2 * step * port

    def inside(place):
        return (place >= 0) & (place < nz)

    def load_g(tile):
        start = pl.multiple_of(tile * width, width)
        return pltpu.make_async_copy(gbar.at[:, pl.ds(start, width)], g_v.at[tile], load_sems.at[tile])

    def load_p(panel):
        columns = slice(panel * width, (panel + 1) * width)
        return pltpu.make_async_copy(panels.at[:, columns], p_v.at[:, columns], load_sems.at[chips + panel])

    def columns_of(side):
        quarter = width // 4
        return {EARLY: slice(0, quarter), LATE: slice(quarter, half), COMB: slice(half, width)}[side]

    def gath(tile, side):
        return gath_comb.at[tile] if side == COMB else gath_spine.at[side // 2, tile]

    def acc(side):
        return acc_comb if side == COMB else acc_spine.at[side // 2]

    def acc_other(side):
        return acc_comb_other if side == COMB else acc_spine_other.at[side // 2]

    def load_own(side):
        return pltpu.make_async_copy(panels.at[:, columns_of(side)], gath(chip, side), own_sems.at[side])

    load_cot = pltpu.make_async_copy(cot, adj_v, load_sems.at[chips + 2])
    load_inv = pltpu.make_async_copy(inverses, inv_v, load_sems.at[chips + 3])

    def order(count):
        place = jnp.where(z < nz // 2, nz - 1 - count // 2, count // 2)
        return 2 * place + jnp.where(count % 2 == 0, 1 - x, x)

    @pl.when(core == col)
    def _():
        for side in (EARLY, COMB, LATE):
            load_own(side).start()

    load_p(1).start()
    for count in range(chips):
        load_g(order(count)).start()
    load_p(0).start()
    load_cot.start()
    load_inv.start()

    barrier = pltpu.get_barrier_semaphore()
    friends = [
        (2 * across + core, col),
        (2 * chip + mate, col),
        (2 * chip + core, 1 - col),
        (2 * chip + mate, 1 - col),
    ]

    def greet(friend):
        pl.semaphore_signal(barrier, inc=1, device_id=friend, device_id_type=MESH)

    for friend in friends:
        greet(friend)
    for port in (UP, DOWN):
        pl.when(has_next(port))(lambda: greet((2 * port_chip(port) + core, col)))

    pl.semaphore_wait(barrier, len(friends) + jnp.where((z > 0) & (z < nz - 1), 2, 1))

    def gather_copy(tile, side, port):
        rows = pl.ds(pl.multiple_of(core * half, half), half)
        return pltpu.make_async_remote_copy(
            gath(tile, side).at[rows],
            gath(tile, side).at[rows],
            gath_send.at[port, tile, side],
            gath_recv.at[tile, side],
            device_id=(2 * port_chip(port) + core, col),
            device_id_type=MESH,
        )

    def gather_pair(tile, side):
        rows = pl.ds(pl.multiple_of(core * half, half), half)
        return pltpu.make_async_remote_copy(
            gath(tile, side).at[rows],
            gath(tile, side).at[rows],
            gath_mate.at[0, tile, side],
            gath_mate.at[1, tile, side],
            device_id=(2 * chip + mate, col),
            device_id_type=MESH,
        )

    def gather_own_pair(side):
        return pltpu.make_async_remote_copy(
            gath(chip, side),
            gath(chip, side),
            gath_mate.at[0, chip, side],
            gath_mate.at[1, chip, side],
            device_id=(2 * chip + mate, col),
            device_id_type=MESH,
        )

    def own_sends(act, routes, sides):
        @pl.when(core == col)
        def _():
            for side in sides:
                act(gather_own_pair(side))

        for side, port in routes:
            if side in sides and act is start:
                @pl.when(core != col)
                def _():
                    gather_own_pair(side).wait_recv()

                sides = tuple(other for other in sides if other != side)
            copy = gather_copy(chip, side, port)
            if port == ACROSS:
                act(copy)
            else:
                pl.when(has_next(port))(lambda: act(copy))

    first_routes = [(EARLY, ACROSS), (COMB, UP), (COMB, DOWN), (EARLY, UP), (EARLY, DOWN), (COMB, ACROSS)]

    def own_first(act):
        own_sends(act, first_routes, (EARLY, COMB))

    def own_across(act):
        own_sends(act, [(LATE, ACROSS)], (LATE,))

    def own_along(act):
        own_sends(act, [(LATE, UP), (LATE, DOWN)], ())

    def relay(tile, side, ports, act):
        for port in ports:
            if port == ACROSS:
                act(gather_copy(tile, side, port))
            else:
                @pl.when(has_next(port))
                def _():
                    act(gather_copy(tile, side, port))
        act(gather_pair(tile, side))

    def arrived(tile, side):
        gather_copy(tile, side, ACROSS).wait_recv()

    def start(copy):
        copy.start()

    def finish(copy):
        copy.wait_send()

    def relay_b(step, act):
        for port in (UP, DOWN):
            place = behind(port, step)

            @pl.when(inside(place))
            def _():
                tile = 2 * place + x
                if act is start:
                    arrived(tile, COMB)
                relay(tile, COMB, (port, ACROSS), act)

    def relay_a(step, act, own, part):
        for port in (UP, DOWN):
            place = behind(port, step)

            @pl.when(inside(place))
            def _():
                tile = 2 * place + (x if own else 1 - x)
                if act is start:
                    arrived(tile, part)
                relay(tile, part, (port,), act)

    def relay_a_across(act, part):
        if act is start:
            arrived(across, part)
        relay(across, part, (UP, DOWN), act)

    def relay_bx(step, act):
        for port in (UP, DOWN) if step else (UP,):
            place = behind(port, step)

            @pl.when(inside(place))
            def _():
                tile = 2 * place + 1 - x
                if act is start:
                    arrived(tile, COMB)
                relay(tile, COMB, (), act)

    def forward(tile, side):
        @pl.when(tile != chip)
        def _():
            gather_pair(tile, side).wait_recv()

        acc(side)[...] += product(halves(g_v[tile]), halves(gath(tile, side)[...]))

    def forward_step(step, kinds):
        def both(port, carry):
            place = behind(port, step)

            @pl.when(inside(place))
            def _():
                for side, own in kinds:
                    forward(2 * place + (x if own else 1 - x), side)

            return carry

        lax.fori_loop(0, 2 if step else 1, both, 0)

    def term_copy(tile):
        return pltpu.make_async_remote_copy(
            terms.at[tile, mate],
            other.at[tile],
            term_sems.at[0, tile],
            term_sems.at[1, tile],
            device_id=(2 * chip + mate, col),
            device_id_type=MESH,
        )

    def xone_copy(place, tile):
        return pltpu.make_async_remote_copy(
            terms.at[tile, core, pl.ds(PAIRED, lane - PAIRED)],
            xin_one.at[place],
            xone_sems.at[0, place],
            xone_sems.at[1, place],
            device_id=(2 * across + core, col),
            device_id_type=MESH,
        )

    def make_terms(count):
        tile = order(count)
        load_g(tile).wait()
        for part in (0, 1):
            rows = slice(part * half, (part + 1) * half)
            value = product((p_high[rows, :], p_low[rows, :]), halves(g_v[tile]))
            terms[tile, part] = value
        term_copy(tile).start()

    def pair_terms(count):
        tile = order(count)
        term_copy(tile).wait_recv()
        terms[tile, core] = terms[tile, core] + other[tile]

        @pl.when(count == 0)
        def _():
            xone_copy(tile // 2, tile).start()

    def send_across(count):
        tile = order(count)
        xone_copy(tile // 2, tile).start()

    def pieces(part, sub):
        size = (lane - PAIRED if part else PAIRED) // SUBS
        start = sub * size if isinstance(sub, int) else pl.multiple_of(sub * size, 8)
        return pl.ds(start, size), pl.ds(start + part * PAIRED, size)

    def pair_copy(port, step, slot, tile, sub):
        rows, _ = pieces(0, sub)
        return pltpu.make_async_remote_copy(
            terms.at[tile, core, rows],
            zin_pair.at[port, step - 1, slot, rows],
            pair_send.at[port, step - 1, slot, sub],
            pair_recv.at[port, step - 1, slot, sub],
            device_id=(2 * port_chip(port) + core, col),
            device_id_type=MESH,
        )

    def one_copy(port, step, tile, sub):
        rows, held = pieces(1, sub)
        return pltpu.make_async_remote_copy(
            terms.at[tile, core, held],
            zin_one.at[port, step - 1, rows],
            one_send.at[port, step - 1, sub],
            one_recv.at[port, step - 1, sub],
            device_id=(2 * port_chip(port) + core, col),
            device_id_type=MESH,
        )

    def sum_pair(step):
        for slot in (0, 1):
            for port in (UP, DOWN):
                place = ahead(port, step)

                @pl.when(inside(place))
                def _():
                    tile = 2 * place + (x if slot else 1 - x)

                    def each(sub, carry):
                        rows, _ = pieces(0, sub)
                        if step < nz - 1:
                            @pl.when(has_prev(port))
                            def _():
                                pair_copy(port, step + 1, slot, tile, sub).wait_recv()
                                terms[tile, core, rows] = (
                                    terms[tile, core, rows] + zin_pair[port, step, slot, rows]
                                )

                        pair_copy(port, step, slot, tile, sub).start()
                        return carry

                    lax.fori_loop(0, SUBS, each, 0)

    def sum_one(step):
        for port in (UP, DOWN):
            place = ahead(port, step)

            @pl.when(inside(place))
            def _():
                tile = 2 * place + x
                xone_copy(place, tile).wait_recv()

                def each(sub, carry):
                    rows, held = pieces(1, sub)
                    value = terms[tile, core, held] + xin_one[place, rows]
                    terms[tile, core, held] = value
                    if step < nz - 1:
                        @pl.when(has_prev(port))
                        def _():
                            one_copy(port, step + 1, tile, sub).wait_recv()
                            terms[tile, core, held] = value + zin_one[port, step, rows]

                    one_copy(port, step, tile, sub).start()
                    return carry

                lax.fori_loop(0, SUBS, each, 0)

    def last_copy(sub):
        rows, _ = pieces(0, sub)
        return pltpu.make_async_remote_copy(
            terms.at[across, core, rows],
            xin_last.at[rows],
            last_sems.at[0, sub],
            last_sems.at[1, sub],
            device_id=(2 * across + core, col),
            device_id_type=MESH,
        )

    def final_rows(part, source_core, sub):
        size = lane - PAIRED if part else PAIRED
        start = source_core * size + sub * (size // SUBS) + (0 if part else split)
        return pl.ds(start if isinstance(start, int) else pl.multiple_of(start, 8), size // SUBS)

    def end_copy(part, plane, source_core, sub):
        _, held = pieces(part, sub)
        return pltpu.make_async_remote_copy(
            terms.at[chip, source_core, held],
            final.at[final_rows(part, source_core, sub)],
            end_send.at[part, plane, sub],
            end_recv.at[part, source_core, sub],
            device_id=(2 * chip + col, col if plane == 0 else 1 - col),
            device_id_type=MESH,
        )

    def end_local(part, source_core, sub):
        _, held = pieces(part, sub)
        return pltpu.make_async_copy(
            terms.at[chip, source_core, held],
            final.at[final_rows(part, source_core, sub)],
            end_recv.at[part, source_core, sub],
        )

    def give_end(part, sub):
        end_copy(part, 1, core, sub).start()

        @pl.when(core == col)
        def _():
            end_local(part, core, sub).start()

        @pl.when(core != col)
        def _():
            end_copy(part, 0, core, sub).start()

    def last_pair(sub, carry):
        rows, _ = pieces(0, sub)
        for slot in (0, 1):
            tile = chip if slot else across
            for port in (UP, DOWN):
                @pl.when(has_prev(port))
                def _():
                    pair_copy(port, 1, slot, tile, sub).wait_recv()
                    terms[tile, core, rows] = terms[tile, core, rows] + zin_pair[port, 0, slot, rows]

            if slot == 0:
                last_copy(sub).start()

        @pl.when(sub > 0)
        def _():
            last_across(sub - 1, carry)

        return carry

    def last_across(sub, carry):
        rows, _ = pieces(0, sub)
        last_copy(sub).wait_recv()
        terms[chip, core, rows] = terms[chip, core, rows] + xin_last[rows]
        give_end(0, sub)
        return carry

    def last_one(sub, carry):
        rows, held = pieces(1, sub)
        terms[chip, core, held] = terms[chip, core, held] + xin_one[z, rows]
        for port in (UP, DOWN):
            @pl.when(has_prev(port))
            def _():
                one_copy(port, 1, chip, sub).wait_recv()
                terms[chip, core, held] = terms[chip, core, held] + zin_one[port, 0, rows]

        give_end(1, sub)
        return carry

    def drain_early():
        own_first(finish)
        own_across(finish)
        own_along(finish)
        relay_a_across(finish, EARLY)
        relay_a_across(finish, LATE)
        relay_bx(0, finish)

        def drain_terms(count, carry):
            tile = order(count)
            term_copy(tile).wait_send()

            @pl.when(tile % 2 != x)
            def _():
                xone_copy(tile // 2, tile).wait_send()

            return carry

        lax.fori_loop(0, chips, drain_terms, 0)
        for step in range(1, nz):
            relay_b(step, finish)
            for part in (EARLY, LATE):
                relay_a(step, finish, True, part)
                relay_a(step, finish, False, part)
            relay_bx(step, finish)

    def drain_step(step):
        def both(port, carry):
            place = ahead(port, step)

            @pl.when(inside(place))
            def _():
                def each(sub, carry):
                    for slot in (0, 1):
                        pair_copy(port, step, slot, 2 * place + (x if slot else 1 - x), sub).wait_send()
                    one_copy(port, step, 2 * place + x, sub).wait_send()
                    return carry

                lax.fori_loop(0, SUBS, each, 0)

            return carry

        lax.fori_loop(0, 2, both, 0)

    def acc_copy(side):
        return pltpu.make_async_remote_copy(
            acc(side),
            acc_other(side),
            acc_sems.at[0, side],
            acc_sems.at[1, side],
            device_id=(2 * chip + core, 1 - col),
            device_id_type=MESH,
        )

    side_columns = pl.ds(pl.multiple_of(col * half, half), half)
    short = width // (2 * chips)

    bound = split // (2 * short)
    groups = ((0, 0, chips), (1, bound, chips), (1, 0, bound))

    def mate_copy(group):
        panel, low, high = groups[group]
        return pltpu.make_async_remote_copy(
            diag_v.at[panel, low:high, mate],
            diag_mate.at[panel, low:high],
            mate_sems.at[0, group],
            mate_sems.at[1, group],
            device_id=(2 * chip + mate, col),
            device_id_type=MESH,
        )

    def part_copy(panel, source, target):
        return pltpu.make_async_remote_copy(
            diag_v.at[panel, target, core],
            diag_parts.at[panel, source],
            part_send.at[panel, target],
            part_recv.at[panel, source],
            device_id=(2 * target + core, col),
            device_id_type=MESH,
        )

    def swap_copy(panel):
        return pltpu.make_async_remote_copy(
            diag_out.at[panel, :, side_columns],
            diag_out.at[panel, :, side_columns],
            swap_sems.at[0, panel],
            swap_sems.at[1, panel],
            device_id=(2 * chip + core, 1 - col),
            device_id_type=MESH,
        )

    def adjoint_out(panel):
        columns = slice(panel * width, (panel + 1) * width)
        return pltpu.make_async_copy(adj_v.at[:, columns], adjoint.at[:, columns], out_sems.at[panel])

    def solve_first():
        for side in (EARLY, COMB, LATE):
            acc_copy(side).wait_recv()
            columns = columns_of(side)
            cot_t[0, :, columns] = adj_v[:, columns] - 2.0 * (acc(side)[...] + acc_other(side)[...])
        turned = product(halves(cot_t[0]), halves(inv_v[0]))
        adj_v[:, :width] = turned
        adjoint_out(0).start()
        cot_t[0] = turned.T

    def wait_end(part):
        for source in (0, 1):
            for sub in range(SUBS):
                end_local(part, source, sub).wait()

    def solve_high():
        wait_end(0)
        cot_t[1, split:] = cot_t[1, split:] - 2.0 * final[split:]
        first = split // 128 * 128
        adj_t[split:] = product(halves(inv_v[1, split:, first:]), halves(cot_t[1, first:]))

    def solve_low():
        wait_end(1)
        cot_t[1, :split] = cot_t[1, :split] - 2.0 * final[:split]
        adj_t[:split] = product(halves(inv_v[1, :split]), halves(cot_t[1]))

    def turn_cot():
        cot_t[1] = adj_v[:, width:].T

    def turn_inv():
        inv_v[1] = inv_v[1].T

    def diagonal(group):
        panel, low, high = groups[group]
        place = pl.multiple_of(panel * width + col * half, half)
        own = p_v[:, pl.ds(place, half)]
        source = adj_t[2 * short * low:2 * short * high] if panel else cot_t[0]
        value = -product(halves(source), halves(own))
        diag_v[panel, low:high] = value.reshape(high - low, 2, short, half)
        mate_copy(group).start()

    def give_second():
        adj_v[:, width:] = adj_t[...].T
        adjoint_out(1).start()

    def scatter(group):
        panel, low, high = groups[group]
        mate_copy(group).wait_recv()
        diag_v[panel, low:high, core] = diag_v[panel, low:high, core] + diag_mate[panel, low:high]
        for hop in range(1, chips):
            target = (chip + hop) % chips

            @pl.when((target >= low) & (target < high))
            def _():
                part_copy(panel, chip, target).start()

    def collect(panel):
        total = diag_v[panel, chip, core]
        for hop in range(1, chips):
            source = (chip + hop) % chips
            part_copy(panel, source, chip).wait_recv()
            total = total + diag_parts[panel, source]
        diag_out[panel, :, side_columns] = total
        swap_copy(panel).start()

    @pl.when(core == col)
    def _():
        for side in (EARLY, COMB, LATE):
            load_own(side).wait()

    own_first(start)
    load_p(1).wait()
    high, low = halves(p_v[:, width:].T)
    for part in (0, 1):
        for to, first, size in (
            (part * half, split + part * PAIRED, PAIRED),
            (part * half + PAIRED, part * (half - PAIRED), half - PAIRED),
        ):
            p_high[to:to + size, :] = high[first:first + size]
            p_low[to:to + size, :] = low[first:first + size]

    acc_spine[...] = jnp.zeros_like(acc_spine)
    acc_comb[...] = jnp.zeros_like(acc_comb)
    chores = {
        3: lambda: (relay_a_across(start, EARLY),)[-1],
        7: lambda: (relay_a(1, start, True, EARLY), relay_b(1, start),)[-1],
    }

    def produce(count, carry):
        make_terms(count)
        pl.when(count > 0)(lambda: pair_terms(count - 1))
        for at, chore in chores.items():
            pl.when(count == at)(chore)
        return carry

    lax.fori_loop(0, chips, produce, 0)
    pair_terms(jnp.int32(chips - 1))

    own_across(start)
    relay_a(1, start, False, EARLY)
    sum_pair(3)
    relay_b(2, start)
    relay_bx(0, start)
    sum_pair(2)
    forward_step(1, [(EARLY, False)])
    relay_a(2, start, True, EARLY)
    send_across(2)
    forward_step(0, [(COMB, True)])
    relay_a(2, start, False, EARLY)
    forward_step(1, [(EARLY, True)])
    forward_step(0, [(COMB, False)])
    forward_step(2, [(EARLY, False), (COMB, True), (EARLY, True)])
    forward_step(0, [(EARLY, False)])
    relay_a_across(start, LATE)
    forward_step(0, [(EARLY, True)])
    relay_b(3, start)
    forward_step(3, [(COMB, True)])
    relay_a(3, start, True, EARLY)
    own_along(start)
    sum_one(3)
    forward_step(3, [(EARLY, True)])
    relay_bx(2, start)
    relay_bx(1, start)
    send_across(6)
    relay_a(3, start, False, EARLY)
    forward_step(3, [(EARLY, False)])
    relay_a(1, start, False, LATE)
    forward_step(1, [(COMB, True)])
    acc_copy(EARLY).start()
    relay_a(1, start, True, LATE)
    forward_step(0, [(LATE, False)])
    forward_step(2, [(COMB, False)])
    forward_step(1, [(COMB, False)])
    sum_one(2)
    relay_bx(3, start)
    forward_step(3, [(COMB, False)])
    acc_copy(COMB).start()
    relay_a(2, start, True, LATE)
    relay_a(2, start, False, LATE)
    forward_step(1, [(LATE, True)])
    send_across(4)
    sum_pair(1)
    forward_step(0, [(LATE, True)])
    forward_step(2, [(LATE, False)])
    relay_a(3, start, True, LATE)
    relay_a(3, start, False, LATE)
    forward_step(3, [(LATE, True)])
    forward_step(2, [(LATE, True)])
    forward_step(3, [(LATE, False)])
    forward_step(1, [(LATE, False)])
    acc_copy(LATE).start()
    sum_one(1)
    load_p(0).wait()
    load_cot.wait()
    load_inv.wait()
    turn_cot()
    turn_inv()
    lax.fori_loop(0, SUBS, last_pair, 0)
    last_across(SUBS - 1, 0)
    solve_first()
    diagonal(0)
    xone_copy(z, chip).wait_recv()
    lax.fori_loop(0, SUBS, last_one, 0)
    scatter(0)
    solve_high()
    diagonal(1)
    scatter(1)
    solve_low()
    diagonal(2)
    scatter(2)
    drain_step(1)
    for sub in range(SUBS):
        last_copy(sub).wait_send()
    for side in (EARLY, COMB, LATE):
        acc_copy(side).wait_send()
    drain_early()
    drain_step(3)
    drain_step(2)
    collect(0)
    give_second()
    collect(1)

    for sub in range(SUBS):
        for part in (0, 1):
            end_copy(part, 1, core, sub).wait_send()

            @pl.when(core != col)
            def _():
                end_copy(part, 0, core, sub).wait_send()

    for group in range(len(groups)):
        mate_copy(group).wait_send()
    for panel in (0, 1):
        for hop in range(1, chips):
            part_copy(panel, chip, (chip + hop) % chips).wait_send()
        swap_copy(panel).wait()
        adjoint_out(panel).wait()
    store = pltpu.make_async_copy(diag_out, diag, out_sems.at[2])
    store.start()
    store.wait()


def ladder_device(gbar, panels, panel_cot, inverses):
    width = inverses.shape[-1]
    chips = lax.axis_size("row") // 2
    nz = chips // 2
    half = width // 2
    short = width // (2 * chips)
    f32, bf16, dma = jnp.float32, jnp.bfloat16, pltpu.SemaphoreType.DMA
    anywhere = pl.BlockSpec(memory_space=pl.ANY)

    def kernel(*refs):
        ladder_kernel(nz, *refs)

    return pl.pallas_call(
        kernel,
        out_shape=(
            jax.ShapeDtypeStruct(panels.shape, f32),
            jax.ShapeDtypeStruct((2, short, width), f32),
        ),
        in_specs=[anywhere] * 4,
        out_specs=(anywhere, anywhere),
        scratch_shapes=[
            pltpu.VMEM((chips, width, width), f32),
            pltpu.VMEM(panels.shape, f32),
            pltpu.VMEM((2, chips, width, width // 4), f32),
            pltpu.VMEM((chips, width, half), f32),
            pltpu.VMEM((chips, 2, half, width), f32),
            pltpu.VMEM((chips, half, width), f32),
            pltpu.VMEM((2, nz - 1, 2, PAIRED, width), f32),
            pltpu.VMEM((2, nz - 1, half - PAIRED, width), f32),
            pltpu.VMEM((nz, half - PAIRED, width), f32),
            pltpu.VMEM((PAIRED, width), f32),
            pltpu.VMEM((width, width), f32),
            pltpu.VMEM((2, width, width // 4), f32),
            pltpu.VMEM((width, half), f32),
            pltpu.VMEM((2, width, width // 4), f32),
            pltpu.VMEM((width, half), f32),
            pltpu.VMEM((width, width), bf16),
            pltpu.VMEM((width, width), bf16),
            pltpu.VMEM(inverses.shape, f32),
            pltpu.VMEM(inverses.shape, f32),
            pltpu.VMEM((width, width), f32),
            pltpu.VMEM(panels.shape, f32),
            pltpu.VMEM((2, chips, 2, short, half), f32),
            pltpu.VMEM((2, chips, short, half), f32),
            pltpu.VMEM((2, chips, short, half), f32),
            pltpu.VMEM((2, short, width), f32),
            dma((chips + 4,)),
            dma((3,)),
            dma((3,)),
            dma((3, chips, 3)),
            dma((chips, 3)),
            dma((2, chips, 3)),
            dma((2, chips)),
            dma((2, nz)),
            dma((2, nz - 1, 2, SUBS)),
            dma((2, nz - 1, 2, SUBS)),
            dma((2, nz - 1, SUBS)),
            dma((2, nz - 1, SUBS)),
            dma((2, SUBS)),
            dma((2, 2, SUBS)),
            dma((2, 2, SUBS)),
            dma((2, 3)),
            dma((2, 3)),
            dma((2, chips)),
            dma((2, chips)),
            dma((2, 2)),
        ],
        compiler_params=pltpu.CompilerParams(
            collective_id=0, has_side_effects=True, vmem_limit_bytes=62 * 1024 * 1024
        ),
    )(gbar, panels, panel_cot, inverses)


def plain_device(gbar, panels, panel_cot, inverses):
    width = inverses.shape[-1]
    mode = lax.Precision.HIGHEST
    row_id = lax.axis_index("row")
    col_count = lax.axis_size("col")
    contract = (((0,), (0,)), ((), ()))
    partial_value = lax.dot_general(
        gbar, panels, contract, precision=mode, preferred_element_type=jnp.float32
    )
    summed = lax.psum(partial_value, "row")
    own_tile = lax.dynamic_slice_in_dim(summed, row_id // col_count * width, width, 0)
    own_tile = jnp.where(lax.axis_index("col") == row_id % col_count, own_tile, 0)
    combined = panel_cot - 2.0 * lax.psum(own_tile, "col")
    adjoint, terms = [], []
    for panel in (0, 1):
        columns = slice(panel * width, (panel + 1) * width)
        adjoint.append(
            jnp.dot(combined[:, columns], inverses[panel], precision=mode, preferred_element_type=jnp.float32)
        )
        terms.append(
            -lax.dot_general(
                adjoint[-1], panels[:, columns], contract, precision=mode, preferred_element_type=jnp.float32
            )
        )
    diag_adjoint = lax.psum_scatter(jnp.stack(terms), "row", scatter_dimension=1, tiled=True)
    return jnp.concatenate(adjoint, axis=1), diag_adjoint


def solution(mesh):
    in_specs = (P("row", "col"), P("row", None), P("row", None), P())
    out_specs = (P("row", None), P(None, "row", None))
    on_ladder = mesh.shape["col"] == 2 and mesh.shape["row"] == 16
    return jax.shard_map(
        ladder_device if on_ladder else plain_device,
        mesh=mesh, in_specs=in_specs, out_specs=out_specs, check_vma=False,
    )
```
